512 devices in a mesh: tm: 16 (over z, core), space: 32 (over y, x).
Axes of the slice: x: 4, y: 8, z: 8, core: 2. Of those that a mesh axis runs over, the one named last changes fastest.
Arguments:
- forward_states: bfloat16 [64, 4, 128, 8, 128], P('tm', None, 'space'), may hold values from -3 to 3
- adjoint_source: float32 [64, 4, 128, 8, 128], P('tm', None, 'space'), may hold values from -6 to 6
- source_gain: float32 [4, 128, 8, 128], P(None, 'space'), may hold values from -4 to 0.3
- guess_pairs: float32 [16, 2, 4, 128, 8, 128], P('tm', None, None, 'space'), may hold values from -6 to 6
Outputs:
- corrected: float32 [16, 2, 4, 128, 8, 128], P('tm', None, None, 'space')
- gradient: float32 [4, 128, 8, 128], P(None, 'space')
The draws below stay inside these ranges and needn't reach their ends.
All inputs are finite; a program needn't handle non-finite values.
Results may differ from the reference program's by a relative error of at most 0.0003.
Values sent between devices are 32-bit elements; how exact they have to be, the bound alone decides.
No kernel may reach another device: no remote copies, remote signals or barrier semaphores. Data moves between devices by JAX's collectives and lax.ppermute only.
A program may use at most 64 MiB of HBM per device.

```python
import jax
import jax.numpy as jnp
from jax import lax

FIELDS = 4
CY = 8
CZ = 128
COARSEN = 4
SWEEPS = 4
STEPS = 64
NX = 128
N_TM = 16


def steps_of(own_key, shape, pieces, low, top_value):
    def one(dim, parts):
        heights = jax.random.uniform(jax.random.fold_in(jax.random.fold_in(own_key, 6), dim), (parts,), jnp.float32, low / len(pieces), top_value / len(pieces))
        return jnp.repeat(jnp.exp(heights), shape[dim] // parts).reshape((-1,) + (1,) * (len(shape) - dim - 1))

    level = one(*pieces[0])
    for cut in pieces[1:]:
        level = level * one(*cut)
    return level


def bell_draw(key, shape, scale, limit, pieces=(), dtype=jnp.bfloat16):
    factor_of = steps_of(key, shape, pieces, -0.22, 0.18) if pieces else 1.0
    values = jax.random.normal(key, shape, jnp.float32) * scale * factor_of
    return jnp.minimum(jnp.maximum(values, -limit), limit).astype(dtype)


def setup_inputs(seed: int = 0) -> dict:
    seeds = jax.random.split(jax.random.key(seed), 5)
    forward_states = bell_draw(seeds[0], (STEPS, FIELDS, NX, CY, CZ), 0.8, 3.0, ((0, 16), (2, 32)))
    adjoint_source = bell_draw(seeds[1], (STEPS, FIELDS, NX, CY, CZ), 1.0, 6.0, ((0, 16), (2, 32)), jnp.float32)
    source_gain = jnp.clip(-4.0 + 4.3 * jax.random.uniform(seeds[2], (FIELDS, NX, CY, CZ), jnp.float32) ** steps_of(seeds[2], (FIELDS, NX, CY, CZ), ((1, 32),), -0.2, 0.2), -4.0, 0.3)
    guess_pairs = bell_draw(seeds[3], (N_TM, 2, FIELDS, NX, CY, CZ), 1.0, 6.0, ((0, 16), (3, 32)), jnp.float32)
    return {"forward_states": forward_states, "adjoint_source": adjoint_source, "source_gain": source_gain, "guess_pairs": guess_pairs}


diffusion = (2.4, 1.2, 0.6, 4.0)
fibre_weight = 128.0
reaction = ((-14.4, 7.2, -4.8, 2.4), (4.8, -19.2, 7.2, -4.8), (-7.2, 2.4, -12.0, 7.2), (4.8, -7.2, 2.4, -38.4))
self_rates = (-14.4, -19.2, -12.0, -38.4)
masses = (1.0, 1.0, 1.0, 0.0)
fine_rate = 3.0
coarse_rate = 0.75
time_step = 0.5
operator_scale = 0.0078125
state_weight = 0.1
gain_weight = 0.25


def column(values):
    return jnp.array(values, jnp.float32).reshape(4, 1, 1, 1)


def from_below(field, axis):
    extent = field.shape[axis]
    retained = lax.slice_in_dim(field, 0, extent - 1, axis=axis)
    widths = [(0, 0)] * field.ndim
    widths[axis] = (1, 0)
    return jnp.pad(retained, widths)


def from_above(field, axis):
    extent = field.shape[axis]
    retained = lax.slice_in_dim(field, 1, extent, axis=axis)
    widths = [(0, 0)] * field.ndim
    widths[axis] = (0, 1)
    return jnp.pad(retained, widths)


def neighbours(field):
    running = fibre_weight * (from_below(field, 1) + from_above(field, 1))
    running = running + from_below(field, 2) + from_above(field, 2)
    return running + from_below(field, 3) + from_above(field, 3)


def coupling(field):
    stacked_rows = []
    for target in range(4):
        running = jnp.zeros_like(field[0])
        for source in range(4):
            if source != target:
                running = running + reaction[source][target] * field[source]
        stacked_rows.append(running)
    return jnp.stack(stacked_rows)


def jacobi_sweep(field, right_side, diagonal):
    spread = column(diffusion) * neighbours(field) + coupling(field)
    return (right_side + operator_scale * spread) / diagonal


def make_diagonal(state, source_gain, rate):
    stencil_total = (2.0 * fibre_weight + 4.0) * column(diffusion)
    spatial = operator_scale * (stencil_total - column(self_rates))
    return rate * column(masses) + spatial + state_weight * state * state - gain_weight * source_gain


def implicit_solve(right_side, diagonal):
    iterate = right_side / diagonal
    for sweep_count in range(SWEEPS):
        iterate = jacobi_sweep(iterate, right_side, diagonal)
    return iterate


def coarse_step(pair, diagonal):
    solved = implicit_solve(column(masses) * (pair[0] - 0.25 * pair[1]), diagonal)
    return jnp.stack([solved, 0.5 * (solved + pair[0])])


def reference(forward_states, adjoint_source, source_gain, guess_pairs):
    states = forward_states.astype(jnp.float32)
    mass = column(masses)
    zero_pair = jnp.zeros_like(guess_pairs[0])
    adjoints = [None] * (COARSEN * N_TM)
    relaxed = []
    for interval in range(N_TM):
        later = guess_pairs[interval + 1] if interval + 1 < N_TM else zero_pair
        ahead_one, ahead_two = later[0], later[1]
        for offset in range(COARSEN - 1, -1, -1):
            position = interval * COARSEN + offset
            diagonal = make_diagonal(states[position], source_gain, fine_rate)
            right_side = adjoint_source[position] + mass * (4.0 * ahead_one - ahead_two)
            current = implicit_solve(right_side, diagonal)
            adjoints[position] = current
            ahead_two, ahead_one = ahead_one, current
        relaxed.append(jnp.stack([adjoints[interval * COARSEN], adjoints[interval * COARSEN + 1]]))
    running = adjoints[0] * states[0]
    for position in range(1, COARSEN * N_TM):
        running = running + adjoints[position] * states[position]
    gradient = time_step * running
    coarse_diags = [make_diagonal(states[interval * COARSEN], source_gain, coarse_rate) for interval in range(N_TM)]
    offsets = []
    for interval in range(N_TM):
        following = relaxed[interval + 1] if interval + 1 < N_TM else zero_pair
        offsets.append(relaxed[interval] - coarse_step(following, coarse_diags[interval]))
    results = [None] * N_TM
    carried = zero_pair
    for interval in range(N_TM - 1, -1, -1):
        carried = coarse_step(carried, coarse_diags[interval]) + offsets[interval]
        results[interval] = carried
    return jnp.stack(results), gradient
```

```python
import jax
import jax.numpy as jnp
from jax import lax
from jax.experimental import pallas as pl
from jax.experimental.pallas import tpu as pltpu
from jax.sharding import PartitionSpec as P

SWEEPS = 4
FIELDS = 4
WIDTH = 4

diffusion = (2.4, 1.2, 0.6, 4.0)
fibre_weight = 128.0
reaction = (
    (-14.4, 7.2, -4.8, 2.4),
    (4.8, -19.2, 7.2, -4.8),
    (-7.2, 2.4, -12.0, 7.2),
    (4.8, -7.2, 2.4, -38.4),
)
self_rates = (-14.4, -19.2, -12.0, -38.4)
masses = (1.0, 1.0, 1.0, 0.0)
fine_rate = 3.0
coarse_rate = 0.75
time_step = 0.5
operator_scale = 0.0078125
state_weight = 0.1
gain_weight = 0.25

AXES = ("tm", "space")
SLAB = (FIELDS, WIDTH, 8, 128)


def column(values):
    return jnp.array(values, jnp.float32).reshape(4, 1, 1, 1)


def make_diagonal(state, source_gain, rate):
    stencil_total = (2.0 * fibre_weight + 4.0) * column(diffusion)
    spatial = operator_scale * (stencil_total - column(self_rates))
    return (
        rate * column(masses) + spatial + state_weight * state * state - gain_weight * source_gain
    )


class Stencil:
    def __init__(self):
        row = lax.broadcasted_iota(jnp.int32, (8, 128), 0)
        lane = lax.broadcasted_iota(jnp.int32, (8, 128), 1)
        self.first_row, self.last_row = row == 0, row == 7
        self.first_lane, self.last_lane = lane == 0, lane == 127

    def cross(self, cell):
        rows = jnp.where(self.first_row, 0.0, pltpu.roll(cell, 1, 0)) + jnp.where(
            self.last_row, 0.0, pltpu.roll(cell, 7, 0)
        )
        lanes = jnp.where(self.first_lane, 0.0, pltpu.roll(cell, 1, 1)) + jnp.where(
            self.last_lane, 0.0, pltpu.roll(cell, 127, 1)
        )
        return rows + lanes

    def sweep(self, below, here, above, start, inverse):
        fresh = []
        for f in range(FIELDS):
            spread = (operator_scale * fibre_weight * diffusion[f]) * (below[f] + above[f])
            spread = spread + (operator_scale * diffusion[f]) * self.cross(here[f])
            for g in range(FIELDS):
                if g != f:
                    spread = spread + (operator_scale * reaction[g][f]) * here[g]
            fresh.append(start[f] + inverse[f] * spread)
        return fresh


def solve(stencil, right, inverse, count, scratch, emit):
    base, ping, pong = scratch
    for layer in range(count):
        for f in range(FIELDS):
            value = right(f, layer)
            if value is None:
                base[f, layer] = jnp.zeros((8, 128), jnp.float32)
            else:
                base[f, layer] = value * inverse(f, layer)
    source = base
    for sweep in range(1, SWEEPS + 1):
        target = ping if sweep % 2 else pong
        for layer in range(sweep, count - sweep):
            below, here, above = (
                [source[f, layer + shift] for f in range(FIELDS)] for shift in (-1, 0, 1)
            )
            start = [base[f, layer] for f in range(FIELDS)]
            factor = [inverse(f, layer) for f in range(FIELDS)]
            fresh = stencil.sweep(below, here, above, start, factor)
            if sweep == SWEEPS:
                emit(layer - SWEEPS, fresh)
            else:
                for f in range(FIELDS):
                    target[f, layer] = fresh[f]
        source = target


def layers_of(pieces):
    return lambda f, layer: pieces[layer // WIDTH][f, layer % WIDTH]


def masses_only(pieces):
    read = layers_of(pieces)
    return lambda f, layer: read(f, layer) if masses[f] else None


def vmem(shape):
    return pltpu.VMEM(shape, jnp.float32)


def call(body, outs, *operands, smem=0, layers=0, flops=0):
    spec = pl.BlockSpec(memory_space=pltpu.VMEM)
    return pl.pallas_call(
        body,
        in_specs=[pl.BlockSpec(memory_space=pltpu.SMEM)] * smem + [spec] * (len(operands) - smem),
        out_specs=[spec] * len(outs),
        out_shape=[jax.ShapeDtypeStruct(shape, jnp.float32) for shape in outs],
        scratch_shapes=[vmem((FIELDS, layers, 8, 128))] * 3,
        compiler_params=pltpu.CompilerParams(vmem_limit_bytes=24 * 1024 * 1024),
        cost_estimate=pl.CostEstimate(flops=flops, bytes_accessed=1 << 20, transcendentals=0),
    )(*operands)


def fine_step(step, right, right_low, right_high, inv, inv_low, inv_high, states, source, previous, total):
    first, last = total is None, step == 0

    def body(*refs):
        refs = list(refs)
        r0, rl, rh, i0, il, ih, u, prev = refs[:8]
        rest = refs[8:]
        src = None if last else rest.pop(0)
        old = None if first else rest.pop(0)
        out, grad = rest[:2]
        more = rest[2:-3]
        scratch = rest[-3:]
        stencil = Stencil()
        right_at = layers_of([rl, r0, rh])
        pieces = [il, i0, ih]

        def inverse(f, layer):
            return pieces[layer // WIDTH][step, f, layer % WIDTH]

        def emit(layer, x):
            for f in range(FIELDS):
                out[f, layer] = x[f]
                term = x[f] * u[f, layer]
                grad[f, layer] = term if first else old[f, layer] + term
                if not last:
                    r = src[f, layer]
                    if masses[f]:
                        r = r + (4.0 * x[f] - prev[f, layer])
                    more[0][f, layer] = r
                else:
                    z3, z6, z7 = more
                    z7[3 + f, layer] = x[f]
                    if masses[f]:
                        z = x[f] - 0.25 * prev[f, layer]
                        z3[f, layer] = z
                        z6[f, layer] = z
                        z7[f, layer] = z
                        z6[3 + f, layer] = x[f]

        solve(stencil, right_at, inverse, 3 * WIDTH, scratch, emit)

    operands = [right, right_low, right_high, inv, inv_low, inv_high, states, previous]
    operands += [] if last else [source]
    operands += [] if first else [total]
    outs = [SLAB, SLAB] + ([carry(3), carry(6), carry(7)] if last else [SLAB])
    return call(body, outs, *operands, layers=3 * WIDTH, flops=28 * 4 * 1024 * 20)


def carry(count):
    return (count, WIDTH, 8, 128)


def offsets_step(z_five, inv_five, inv_three, own_three, pair_odd, pair_even):
    def body(*refs):
        z, iv, ie, zo, (x0, x1, even) = refs[0:5], refs[5:10], refs[10], refs[11:14], refs[14:17]
        v, pairs = refs[17:19]
        scratch = refs[19:]
        stencil = Stencil()

        def emit_odd(layer, q):
            slab, at = layer // WIDTH, layer % WIDTH
            for f in range(FIELDS):
                if masses[f]:
                    v[f, layer] = zo[slab][f, at] - 0.875 * q[f] + 0.125 * z[slab + 1][3 + f, at]
                if slab == 1:
                    pairs[0, 0, f, at] = x0[f, at] - q[f]
                    pairs[0, 1, f, at] = x1[f, at] - 0.5 * (q[f] + z[2][3 + f, at])

        def emit_even(layer, q):
            for f in range(FIELDS):
                pairs[1, 0, f, layer] = even[0, f, layer] - q[f]
                pairs[1, 1, f, layer] = even[1, f, layer] - 0.5 * (q[f] + x0[f, layer])

        inv_at = lambda f, layer: ie[layer // WIDTH, f, layer % WIDTH]
        solve(stencil, masses_only(z), layers_of(iv), 5 * WIDTH, scratch, emit_odd)
        solve(stencil, masses_only(zo), inv_at, 3 * WIDTH, scratch, emit_even)

    return call(
        body,
        [(3, 3 * WIDTH, 8, 128), (2, 2) + SLAB],
        *z_five, *inv_five, inv_three, *own_three, *pair_odd, pair_even,
        layers=5 * WIDTH, flops=88 * 4 * 1024 * 20,
    )


def chip_step(turn, place, z_five, inv_five, inv_three, v_three, offsets, done, grad):
    with_done, with_grad, with_z = done is not None, grad is not None, z_five is not None

    def body(*refs):
        refs = list(refs)
        spot = refs.pop(0)
        z = [refs.pop(0) for _ in range(5)] if with_z else None
        iv = [refs.pop(0) for _ in range(5)]
        ie, v, o = refs.pop(0), refs.pop(0), refs.pop(0)
        before = refs.pop(0) if with_done else None
        g = [refs.pop(0) for _ in range(2)] if with_grad else None
        z3, z6, z7, pairs = refs[:4]
        sums = refs[4] if with_grad else None
        middle, scratch = refs[-4], refs[-3:]
        if with_grad:
            sums[...] = g[0][...] + g[1][...]
        mine = spot[0] == turn

        @pl.when(jnp.logical_not(mine))
        def _():
            pairs[...] = before[...] if with_done else jnp.zeros_like(pairs)
            z3[...] = jnp.zeros_like(z3)
            z6[...] = jnp.zeros_like(z6)
            z7[...] = jnp.zeros_like(z7)

        @pl.when(mine)
        def _():
            stencil = Stencil()
            zero = jnp.zeros((8, 128), jnp.float32)

            def emit_odd(layer, q):
                slab, at = layer // WIDTH, layer % WIDTH
                for f in range(FIELDS):
                    own = slab == 1
                    c0 = z[slab + 1][3 + f, at] if with_z and (own or masses[f]) else zero
                    if masses[f]:
                        middle[f, layer] = 0.875 * q[f] - 0.125 * c0 + v[f, layer]
                    if own:
                        pairs[0, 0, f, at] = q[f] + o[0, 0, f, at]
                        pairs[0, 1, f, at] = 0.5 * (q[f] + c0) + o[0, 1, f, at]

            def emit_even(layer, q):
                for f in range(FIELDS):
                    c0 = q[f] + o[1, 0, f, layer]
                    c1 = 0.5 * (q[f] + pairs[0, 0, f, layer]) + o[1, 1, f, layer]
                    pairs[1, 0, f, layer] = c0
                    pairs[1, 1, f, layer] = c1
                    z7[3 + f, layer] = c0
                    if masses[f]:
                        carried = c0 - 0.25 * c1
                        z3[f, layer] = carried
                        z6[f, layer] = carried
                        z7[f, layer] = carried
                        z6[3 + f, layer] = c0

            if with_z:
                right = masses_only(z)
            else:
                right = lambda f, layer: zero if masses[f] else None
            middle_at = lambda f, layer: middle[f, layer] if masses[f] else None
            inv_at = lambda f, layer: ie[layer // WIDTH, f, layer % WIDTH]
            solve(stencil, right, layers_of(iv), 5 * WIDTH, scratch, emit_odd)
            solve(stencil, middle_at, inv_at, 3 * WIDTH, scratch, emit_even)

    spec = pl.BlockSpec(memory_space=pltpu.VMEM)
    operands = [place] + (list(z_five) if with_z else []) + list(inv_five) + [inv_three, v_three, offsets]
    operands += [done] if with_done else []
    operands += list(grad) if with_grad else []
    outs = [carry(3), carry(6), carry(7), (2, 2) + SLAB] + ([SLAB] if with_grad else [])
    return pl.pallas_call(
        body,
        in_specs=[pl.BlockSpec(memory_space=pltpu.SMEM)] + [spec] * (len(operands) - 1),
        out_specs=[spec] * len(outs),
        out_shape=[jax.ShapeDtypeStruct(shape, jnp.float32) for shape in outs],
        scratch_shapes=[vmem((3, 3 * WIDTH, 8, 128))] + [vmem((FIELDS, 5 * WIDTH, 8, 128))] * 3,
        compiler_params=pltpu.CompilerParams(vmem_limit_bytes=24 * 1024 * 1024),
        cost_estimate=pl.CostEstimate(flops=88 * 4 * 1024 * 20, bytes_accessed=1 << 20, transcendentals=0),
    )(*operands)


def routes(times, slabs, moved, chosen=None):
    pairs = []
    for k in range(times):
        for s in range(slabs):
            target = moved(k, s)
            if target is None or (chosen is not None and not chosen(k)):
                continue
            k2, s2 = target
            if 0 <= k2 < times and 0 <= s2 < slabs:
                pairs.append((k * slabs + s, k2 * slabs + s2))
    return pairs


def send(value, pairs):
    return lax.ppermute(value, AXES, pairs)


def program(times, slabs):
    chips = times // 2

    def shift(count):
        return routes(times, slabs, lambda k, s: (k, s + count))

    right_one, left_one, right_two, left_two = shift(1), shift(-1), shift(2), shift(-2)
    earlier = routes(times, slabs, lambda k, s: (k - 1, s))
    even_to_odd = routes(times, slabs, lambda k, s: (k + 1, s), lambda k: k % 2 == 0)
    odd_to_even = routes(times, slabs, lambda k, s: (k - 1, s), lambda k: k % 2 == 1)
    reach = (2, 1, 0, -1, -2)
    relaxed_routes = [
        routes(times, slabs, lambda k, s, d=d: (k - 1, s + d), lambda k: k % 2 == 0) for d in reach
    ]

    def hop_routes(hop):
        group = [h for h in range(1, chips) if (h - hop) % 4 == 0]
        senders = [2 * (chips - h) + 1 for h in group]
        return [
            routes(times, slabs, lambda k, s, d=d: (k - 2, s + d), lambda k: k in senders)
            for d in reach
        ]

    def on_device(forward_states, adjoint_source, source_gain, guess_pairs):
        states = forward_states.astype(jnp.float32)
        inverses = jnp.stack(
            [1.0 / make_diagonal(states[n], source_gain, fine_rate) for n in range(4)]
            + [1.0 / make_diagonal(states[0], source_gain, coarse_rate)]
        )
        ahead = send(guess_pairs[0], earlier)
        inv_low, inv_high = send(inverses, right_one), send(inverses, left_one)
        right = adjoint_source[3] + column(masses) * (4.0 * ahead[0] - ahead[1])
        coarse = inverses[4]
        coarse_low2, coarse_high2 = send(coarse, right_two), send(coarse, left_two)
        inv_five = [coarse_low2, inv_low[4], coarse, inv_high[4], coarse_high2]
        inv_three = send(jnp.stack([inv_low[4], coarse, inv_high[4]]), even_to_odd)

        previous, total = ahead[0], None
        adjoints = [None] * 4
        for n in (3, 2, 1, 0):
            low, high = send(right, right_one), send(right, left_one)
            source = adjoint_source[n - 1] if n else None
            x, total, *more = fine_step(
                n, right, low, high, inverses, inv_low, inv_high, states[n], source, previous, total
            )
            adjoints[n] = x
            previous = x
            if n:
                right = more[0]
        z3, z6, z7 = more
        total = time_step * total

        z_low, z_high = send(z3, right_one), send(z3, left_one)
        pair_even = send(jnp.stack([adjoints[0], adjoints[1]]), even_to_odd)
        payload = (z3, z6, z7, z6, z3)
        z_five = [send(part, path) for part, path in zip(payload, relaxed_routes)]
        v, offsets = offsets_step(
            z_five, inv_five, inv_three, (z_low, z3, z_high), (adjoints[0], adjoints[1]), pair_even
        )

        place = (lax.axis_index("tm").astype(jnp.int32)).reshape(1)
        stages = []
        far = 1
        while far < chips:
            stages.append(
                routes(times, slabs, lambda k, s, d=far: (2 * ((k // 2) ^ d), s), lambda k: k % 2 == 0)
            )
            far *= 2
        stages = [odd_to_even] + stages
        z_five, done, grad, hop = None, None, total, 0
        while hop < chips or stages:
            added = None
            if hop and stages:
                added = (grad, send(grad, stages.pop(0)))
            if hop < chips:
                if hop:
                    z_five = [send(part, path) for part, path in zip(payload, hop_routes(hop))]
                z3, z6, z7, done, *sums = chip_step(
                    times - 1 - 2 * hop, place, z_five, inv_five, inv_three, v, offsets, done, added
                )
                payload = (z3, z6, z7, z6, z3)
                if sums:
                    grad = sums[0]
            elif added:
                grad = added[0] + added[1]
            hop += 1

        even = lax.axis_index("tm") % 2 == 0
        grad_odd = send(grad, even_to_odd)
        gradient = jnp.where(even, grad, grad_odd)
        done_even = send(done[1], odd_to_even)
        corrected = jnp.where(even, done_even, done[0])
        return corrected[None], gradient

    return on_device


def solution(mesh):
    placed = (
        P("tm", None, "space", None, None),
        P("tm", None, "space", None, None),
        P(None, "space", None, None),
        P("tm", None, None, "space", None, None),
    )
    return jax.shard_map(
        program(mesh.shape["tm"], mesh.shape["space"]),
        mesh=mesh,
        in_specs=placed,
        out_specs=(P("tm", None, None, "space", None, None), P(None, "space", None, None)),
        check_vma=False,
    )
```

```python
import jax
import jax.numpy as jnp
from jax import lax
from jax.experimental import pallas as pl
from jax.experimental.pallas import tpu as pltpu
from jax.sharding import PartitionSpec as P

SWEEPS = 4
FIELDS = 4
WIDTH = 4

diffusion = (2.4, 1.2, 0.6, 4.0)
fibre_weight = 128.0
reaction = (
    (-14.4, 7.2, -4.8, 2.4),
    (4.8, -19.2, 7.2, -4.8),
    (-7.2, 2.4, -12.0, 7.2),
    (4.8, -7.2, 2.4, -38.4),
)
self_rates = (-14.4, -19.2, -12.0, -38.4)
masses = (1.0, 1.0, 1.0, 0.0)
fine_rate = 3.0
coarse_rate = 0.75
time_step = 0.5
operator_scale = 0.0078125
state_weight = 0.1
gain_weight = 0.25

AXES = ("tm", "space")
SLAB = (FIELDS, WIDTH, 8, 128)


def column(values):
    return jnp.array(values, jnp.float32).reshape(4, 1, 1, 1)


def make_diagonal(state, source_gain, rate):
    stencil_total = (2.0 * fibre_weight + 4.0) * column(diffusion)
    spatial = operator_scale * (stencil_total - column(self_rates))
    return (
        rate * column(masses) + spatial + state_weight * state * state - gain_weight * source_gain
    )


class Stencil:
    def __init__(self):
        row = lax.broadcasted_iota(jnp.int32, (8, 128), 0)
        lane = lax.broadcasted_iota(jnp.int32, (8, 128), 1)
        self.first_row, self.last_row = row == 0, row == 7
        self.first_lane, self.last_lane = lane == 0, lane == 127

    def cross(self, cell):
        rows = jnp.where(self.first_row, 0.0, pltpu.roll(cell, 1, 0)) + jnp.where(
            self.last_row, 0.0, pltpu.roll(cell, 7, 0)
        )
        lanes = jnp.where(self.first_lane, 0.0, pltpu.roll(cell, 1, 1)) + jnp.where(
            self.last_lane, 0.0, pltpu.roll(cell, 127, 1)
        )
        return rows + lanes

    def sweep(self, below, here, above, start, inverse):
        fresh = []
        for f in range(FIELDS):
            spread = (operator_scale * fibre_weight * diffusion[f]) * (below[f] + above[f])
            spread = spread + (operator_scale * diffusion[f]) * self.cross(here[f])
            for g in range(FIELDS):
                if g != f:
                    spread = spread + (operator_scale * reaction[g][f]) * here[g]
            fresh.append(start[f] + inverse[f] * spread)
        return fresh


def solve(stencil, right, inverse, count, scratch, emit):
    base, ping, pong = scratch
    for layer in range(count):
        for f in range(FIELDS):
            value = right(f, layer)
            if value is None:
                base[f, layer] = jnp.zeros((8, 128), jnp.float32)
            else:
                base[f, layer] = value * inverse(f, layer)
    source = base
    for sweep in range(1, SWEEPS + 1):
        target = ping if sweep % 2 else pong
        for layer in range(sweep, count - sweep):
            below, here, above = (
                [source[f, layer + shift] for f in range(FIELDS)] for shift in (-1, 0, 1)
            )
            start = [base[f, layer] for f in range(FIELDS)]
            factor = [inverse(f, layer) for f in range(FIELDS)]
            fresh = stencil.sweep(below, here, above, start, factor)
            if sweep == SWEEPS:
                emit(layer - SWEEPS, fresh)
            else:
                for f in range(FIELDS):
                    target[f, layer] = fresh[f]
        source = target


def layers_of(pieces):
    return lambda f, layer: pieces[layer // WIDTH][f, layer % WIDTH]


def masses_only(pieces):
    read = layers_of(pieces)
    return lambda f, layer: read(f, layer) if masses[f] else None


def vmem(shape):
    return pltpu.VMEM(shape, jnp.float32)


def call(body, outs, *operands, smem=0, layers=0, flops=0):
    spec = pl.BlockSpec(memory_space=pltpu.VMEM)
    return pl.pallas_call(
        body,
        in_specs=[pl.BlockSpec(memory_space=pltpu.SMEM)] * smem + [spec] * (len(operands) - smem),
        out_specs=[spec] * len(outs),
        out_shape=[jax.ShapeDtypeStruct(shape, jnp.float32) for shape in outs],
        scratch_shapes=[vmem((FIELDS, layers, 8, 128))] * 3,
        compiler_params=pltpu.CompilerParams(vmem_limit_bytes=24 * 1024 * 1024),
        cost_estimate=pl.CostEstimate(flops=flops, bytes_accessed=1 << 20, transcendentals=0),
    )(*operands)


def fine_step(step, right, right_low, right_high, inv, inv_low, inv_high, states, source, previous, total):
    first, last = total is None, step == 0

    def body(*refs):
        refs = list(refs)
        r0, rl, rh, i0, il, ih, u, prev = refs[:8]
        rest = refs[8:]
        src = None if last else rest.pop(0)
        old = None if first else rest.pop(0)
        out, grad = rest[:2]
        more = rest[2:-3]
        scratch = rest[-3:]
        stencil = Stencil()
        right_at = layers_of([rl, r0, rh])
        pieces = [il, i0, ih]

        def inverse(f, layer):
            return pieces[layer // WIDTH][step, f, layer % WIDTH]

        def emit(layer, x):
            for f in range(FIELDS):
                out[f, layer] = x[f]
                term = x[f] * u[f, layer]
                grad[f, layer] = term if first else old[f, layer] + term
                if not last:
                    r = src[f, layer]
                    if masses[f]:
                        r = r + (4.0 * x[f] - prev[f, layer])
                    more[0][f, layer] = r
                    if first:
                        more[1][f, layer] = r
                else:
                    z7, pack = more
                    z7[3 + f, layer] = x[f]
                    pack[0, f, layer] = x[f]
                    pack[1, f, layer] = prev[f, layer]
                    if masses[f]:
                        z7[f, layer] = x[f] - 0.25 * prev[f, layer]

        if first:
            more[0][FIELDS:] = il[4]
            more[1][FIELDS:] = ih[4]
        if last:
            for place in range(3):
                more[1][2 + place] = pieces[place][4]
        solve(stencil, right_at, inverse, 3 * WIDTH, scratch, emit)

    operands = [right, right_low, right_high, inv, inv_low, inv_high, states, previous]
    operands += [] if last else [source]
    operands += [] if first else [total]
    outs = [SLAB, SLAB]
    outs += [carry(7), (5,) + SLAB] if last else [carry(8)] * 2 if first else [SLAB]
    return call(body, outs, *operands, layers=3 * WIDTH, flops=28 * 4 * 1024 * 20)


def carry(count):
    return (count, WIDTH, 8, 128)


def offsets_step(z_three, inv_five, pack, own_three, pair_odd):
    def body(*refs):
        (zl, zm, zh), iv, even, zo, (x0, x1) = refs[0:3], refs[3:8], refs[8], refs[9:12], refs[12:14]
        v, pairs = refs[14:16]
        scratch = refs[16:]
        z = [zl.at[0:3], zl.at[3:9], zm, zh.at[0:6], zh.at[6:9]]
        stencil = Stencil()

        def emit_odd(layer, q):
            slab, at = layer // WIDTH, layer % WIDTH
            for f in range(FIELDS):
                if masses[f]:
                    v[f, layer] = zo[slab][f, at] - 0.875 * q[f] + 0.125 * z[slab + 1][3 + f, at]
                if slab == 1:
                    pairs[0, 0, f, at] = x0[f, at] - q[f]
                    pairs[0, 1, f, at] = x1[f, at] - 0.5 * (q[f] + z[2][3 + f, at])

        def emit_even(layer, q):
            for f in range(FIELDS):
                pairs[1, 0, f, layer] = even[0, f, layer] - q[f]
                pairs[1, 1, f, layer] = even[1, f, layer] - 0.5 * (q[f] + x0[f, layer])

        inv_at = lambda f, layer: even[2 + layer // WIDTH, f, layer % WIDTH]
        solve(stencil, masses_only(z), layers_of(iv), 5 * WIDTH, scratch, emit_odd)
        solve(stencil, masses_only(zo), inv_at, 3 * WIDTH, scratch, emit_even)

    return call(
        body,
        [(3, 3 * WIDTH, 8, 128), (2, 2) + SLAB],
        *z_three, *inv_five, pack, *own_three, *pair_odd,
        layers=5 * WIDTH, flops=88 * 4 * 1024 * 20,
    )


def chip_step(turn, place, z_five, inv_five, pack, v_three, offsets, done, grad):
    with_done, with_grad, with_z = done is not None, grad is not None, z_five is not None

    def body(*refs):
        refs = list(refs)
        spot = refs.pop(0)
        z = [refs.pop(0) for _ in range(5)] if with_z else None
        iv = [refs.pop(0) for _ in range(5)]
        even, v, o = refs.pop(0), refs.pop(0), refs.pop(0)
        before = refs.pop(0) if with_done else None
        g = [refs.pop(0) for _ in range(2)] if with_grad else None
        z3, z6, z7, pairs = refs[:4]
        sums = refs[4] if with_grad else None
        middle, scratch = refs[-4], refs[-3:]
        if with_grad:
            sums[...] = g[0][...] + g[1][...]
        mine = spot[0] == turn

        @pl.when(jnp.logical_not(mine))
        def _():
            pairs[...] = before[...] if with_done else jnp.zeros_like(pairs)
            z3[...] = jnp.zeros_like(z3)
            z6[...] = jnp.zeros_like(z6)
            z7[...] = jnp.zeros_like(z7)

        @pl.when(mine)
        def _():
            stencil = Stencil()
            zero = jnp.zeros((8, 128), jnp.float32)

            def emit_odd(layer, q):
                slab, at = layer // WIDTH, layer % WIDTH
                for f in range(FIELDS):
                    own = slab == 1
                    c0 = z[slab + 1][3 + f, at] if with_z and (own or masses[f]) else zero
                    if masses[f]:
                        middle[f, layer] = 0.875 * q[f] - 0.125 * c0 + v[f, layer]
                    if own:
                        pairs[0, 0, f, at] = q[f] + o[0, 0, f, at]
                        pairs[0, 1, f, at] = 0.5 * (q[f] + c0) + o[0, 1, f, at]

            def emit_even(layer, q):
                for f in range(FIELDS):
                    c0 = q[f] + o[1, 0, f, layer]
                    c1 = 0.5 * (q[f] + pairs[0, 0, f, layer]) + o[1, 1, f, layer]
                    pairs[1, 0, f, layer] = c0
                    pairs[1, 1, f, layer] = c1
                    z7[3 + f, layer] = c0
                    if masses[f]:
                        carried = c0 - 0.25 * c1
                        z3[f, layer] = carried
                        z6[f, layer] = carried
                        z7[f, layer] = carried
                        z6[3 + f, layer] = c0

            if with_z:
                right = masses_only(z)
            else:
                right = lambda f, layer: zero if masses[f] else None
            middle_at = lambda f, layer: middle[f, layer] if masses[f] else None
            inv_at = lambda f, layer: even[2 + layer // WIDTH, f, layer % WIDTH]
            solve(stencil, right, layers_of(iv), 5 * WIDTH, scratch, emit_odd)
            solve(stencil, middle_at, inv_at, 3 * WIDTH, scratch, emit_even)

    spec = pl.BlockSpec(memory_space=pltpu.VMEM)
    operands = [place] + (list(z_five) if with_z else []) + list(inv_five) + [pack, v_three, offsets]
    operands += [done] if with_done else []
    operands += list(grad) if with_grad else []
    outs = [carry(3), carry(6), carry(7), (2, 2) + SLAB] + ([SLAB] if with_grad else [])
    return pl.pallas_call(
        body,
        in_specs=[pl.BlockSpec(memory_space=pltpu.SMEM)] + [spec] * (len(operands) - 1),
        out_specs=[spec] * len(outs),
        out_shape=[jax.ShapeDtypeStruct(shape, jnp.float32) for shape in outs],
        scratch_shapes=[vmem((3, 3 * WIDTH, 8, 128))] + [vmem((FIELDS, 5 * WIDTH, 8, 128))] * 3,
        compiler_params=pltpu.CompilerParams(vmem_limit_bytes=24 * 1024 * 1024),
        cost_estimate=pl.CostEstimate(flops=88 * 4 * 1024 * 20, bytes_accessed=1 << 20, transcendentals=0),
    )(*operands)


def routes(times, slabs, moved, chosen=None):
    pairs = []
    for k in range(times):
        for s in range(slabs):
            target = moved(k, s)
            if target is None or (chosen is not None and not chosen(k)):
                continue
            k2, s2 = target
            if 0 <= k2 < times and 0 <= s2 < slabs:
                pairs.append((k * slabs + s, k2 * slabs + s2))
    return pairs


def send(value, pairs):
    return lax.ppermute(value, AXES, pairs)


def program(times, slabs):
    chips = times // 2

    def shift(count):
        return routes(times, slabs, lambda k, s: (k, s + count))

    right_one, left_one = shift(1), shift(-1)
    earlier = routes(times, slabs, lambda k, s: (k - 1, s))
    even_to_odd = routes(times, slabs, lambda k, s: (k + 1, s), lambda k: k % 2 == 0)
    odd_to_even = routes(times, slabs, lambda k, s: (k - 1, s), lambda k: k % 2 == 1)
    reach = (2, 1, 0, -1, -2)
    relaxed_routes = [
        routes(times, slabs, lambda k, s, d=d: (k - 1, s + d), lambda k: k % 2 == 0) for d in (1, 0, -1)
    ]

    def hop_routes(hop):
        group = [h for h in range(1, chips) if (h - hop) % 4 == 0]
        senders = [2 * (chips - h) + 1 for h in group]
        return [
            routes(times, slabs, lambda k, s, d=d: (k - 2, s + d), lambda k: k in senders)
            for d in reach
        ]

    def on_device(forward_states, adjoint_source, source_gain, guess_pairs):
        states = forward_states.astype(jnp.float32)
        inverses = jnp.stack(
            [1.0 / make_diagonal(states[n], source_gain, fine_rate) for n in range(4)]
            + [1.0 / make_diagonal(states[0], source_gain, coarse_rate)]
        )
        ahead = send(guess_pairs[0], earlier)
        inv_low, inv_high = send(inverses, right_one), send(inverses, left_one)
        right = adjoint_source[3] + column(masses) * (4.0 * ahead[0] - ahead[1])
        previous, total = ahead[0], None
        adjoints = [None] * 4
        for n in (3, 2, 1, 0):
            if n == 2:
                low, high = send(more[0], right_one), send(more[1], left_one)
                inv_five = [low[FIELDS:], inv_low[4], inverses[4], inv_high[4], high[FIELDS:]]
            else:
                low, high = send(right, right_one), send(right, left_one)
            source = adjoint_source[n - 1] if n else None
            x, total, *more = fine_step(
                n, right, low, high, inverses, inv_low, inv_high, states[n], source, previous, total
            )
            adjoints[n] = x
            previous = x
            if n:
                right = more[0]
        z7, pack = more
        total = time_step * total

        z_low, z_high = send(z7, right_one), send(z7, left_one)
        pack = send(pack, even_to_odd)
        payload = (
            jnp.concatenate([z_low[:3], z7[:6]]), z7, jnp.concatenate([z7[:6], z_high[:3]])
        )
        z_three = [send(part, path) for part, path in zip(payload, relaxed_routes)]
        v, offsets = offsets_step(
            z_three, inv_five, pack, (z_low, z7, z_high), (adjoints[0], adjoints[1])
        )

        place = (lax.axis_index("tm").astype(jnp.int32)).reshape(1)
        stages = []
        far = 1
        while far < chips:
            stages.append(
                routes(times, slabs, lambda k, s, d=far: (2 * ((k // 2) ^ d), s), lambda k: k % 2 == 0)
            )
            far *= 2
        stages = [odd_to_even] + stages
        z_five, done, grad, hop = None, None, total, 0
        while hop < chips or stages:
            added = None
            if hop and hop < chips:
                z_five = [send(part, path) for part, path in zip(payload, hop_routes(hop))]
            if hop and stages:
                arrived = sum(part[0, 0, 0, 0] for part in z_five)
                late = jnp.where(place[0] < 0, arrived, grad)
                added = (grad, send(late, stages.pop(0)))
            if hop < chips:
                z3, z6, z7, done, *sums = chip_step(
                    times - 1 - 2 * hop, place, z_five, inv_five, pack, v, offsets, done, added
                )
                payload = (z3, z6, z7, z6, z3)
                if sums:
                    grad = sums[0]
            elif added:
                grad = added[0] + added[1]
            hop += 1

        even = lax.axis_index("tm") % 2 == 0
        grad_odd = send(grad, even_to_odd)
        gradient = jnp.where(even, grad, grad_odd)
        done_even = send(done[1], odd_to_even)
        corrected = jnp.where(even, done_even, done[0])
        return corrected[None], gradient

    return on_device


def solution(mesh):
    placed = (
        P("tm", None, "space", None, None),
        P("tm", None, "space", None, None),
        P(None, "space", None, None),
        P("tm", None, None, "space", None, None),
    )
    return jax.shard_map(
        program(mesh.shape["tm"], mesh.shape["space"]),
        mesh=mesh,
        in_specs=placed,
        out_specs=(P("tm", None, None, "space", None, None), P(None, "space", None, None)),
        check_vma=False,
    )
```

```python
import jax
import jax.numpy as jnp
from jax import lax
from jax.experimental import pallas as pl
from jax.experimental.pallas import tpu as pltpu
from jax.sharding import PartitionSpec as P

SWEEPS = 4
FIELDS = 4
WIDTH = 4

diffusion = (2.4, 1.2, 0.6, 4.0)
fibre_weight = 128.0
reaction = (
    (-14.4, 7.2, -4.8, 2.4),
    (4.8, -19.2, 7.2, -4.8),
    (-7.2, 2.4, -12.0, 7.2),
    (4.8, -7.2, 2.4, -38.4),
)
self_rates = (-14.4, -19.2, -12.0, -38.4)
masses = (1.0, 1.0, 1.0, 0.0)
fine_rate = 3.0
coarse_rate = 0.75
time_step = 0.5
operator_scale = 0.0078125
state_weight = 0.1
gain_weight = 0.25

AXES = ("tm", "space")
SLAB = (FIELDS, WIDTH, 8, 128)


def column(values):
    return jnp.array(values, jnp.float32).reshape(4, 1, 1, 1)


def make_diagonal(state, source_gain, rate):
    stencil_total = (2.0 * fibre_weight + 4.0) * column(diffusion)
    spatial = operator_scale * (stencil_total - column(self_rates))
    return (
        rate * column(masses) + spatial + state_weight * state * state - gain_weight * source_gain
    )


class Stencil:
    def __init__(self):
        row = lax.broadcasted_iota(jnp.int32, (8, 128), 0)
        lane = lax.broadcasted_iota(jnp.int32, (8, 128), 1)
        self.first_row, self.last_row = row == 0, row == 7
        self.first_lane, self.last_lane = lane == 0, lane == 127

    def cross(self, cell):
        rows = jnp.where(self.first_row, 0.0, pltpu.roll(cell, 1, 0)) + jnp.where(
            self.last_row, 0.0, pltpu.roll(cell, 7, 0)
        )
        lanes = jnp.where(self.first_lane, 0.0, pltpu.roll(cell, 1, 1)) + jnp.where(
            self.last_lane, 0.0, pltpu.roll(cell, 127, 1)
        )
        return rows + lanes

    def sweep(self, below, here, above, start, inverse):
        fresh = []
        for f in range(FIELDS):
            spread = (operator_scale * fibre_weight * diffusion[f]) * (below[f] + above[f])
            spread = spread + (operator_scale * diffusion[f]) * self.cross(here[f])
            for g in range(FIELDS):
                if g != f:
                    spread = spread + (operator_scale * reaction[g][f]) * here[g]
            fresh.append(start[f] + inverse[f] * spread)
        return fresh


def solve(stencil, right, inverse, count, scratch, emit):
    base, ping, pong = scratch
    for layer in range(count):
        for f in range(FIELDS):
            value = right(f, layer)
            if value is None:
                base[f, layer] = jnp.zeros((8, 128), jnp.float32)
            else:
                base[f, layer] = value * inverse(f, layer)
    source = base
    for sweep in range(1, SWEEPS + 1):
        target = ping if sweep % 2 else pong
        for layer in range(sweep, count - sweep):
            below, here, above = (
                [source[f, layer + shift] for f in range(FIELDS)] for shift in (-1, 0, 1)
            )
            start = [base[f, layer] for f in range(FIELDS)]
            factor = [inverse(f, layer) for f in range(FIELDS)]
            fresh = stencil.sweep(below, here, above, start, factor)
            if sweep == SWEEPS:
                emit(layer - SWEEPS, fresh)
            else:
                for f in range(FIELDS):
                    target[f, layer] = fresh[f]
        source = target


def layers_of(pieces):
    return lambda f, layer: pieces[layer // WIDTH][f, layer % WIDTH]


def masses_only(pieces):
    read = layers_of(pieces)
    return lambda f, layer: read(f, layer) if masses[f] else None


def vmem(shape):
    return pltpu.VMEM(shape, jnp.float32)


def call(body, outs, *operands, smem=0, layers=0, flops=0):
    spec = pl.BlockSpec(memory_space=pltpu.VMEM)
    return pl.pallas_call(
        body,
        in_specs=[pl.BlockSpec(memory_space=pltpu.SMEM)] * smem + [spec] * (len(operands) - smem),
        out_specs=[spec] * len(outs),
        out_shape=[jax.ShapeDtypeStruct(shape, jnp.float32) for shape in outs],
        scratch_shapes=[vmem((FIELDS, layers, 8, 128))] * 3,
        compiler_params=pltpu.CompilerParams(vmem_limit_bytes=24 * 1024 * 1024),
        cost_estimate=pl.CostEstimate(flops=flops, bytes_accessed=1 << 20, transcendentals=0),
    )(*operands)


def fine_step(step, own, low, high, states, previous, total, source=None, factor=None, coarse=None):
    first, second, last = total is None, step == 2, step == 0

    def body(*refs):
        refs = list(refs)
        r0, rl, rh, u, prev = [refs.pop(0) for _ in range(5)]
        src, inv = (None, None) if last else [refs.pop(0) for _ in range(2)]
        factors = [refs.pop(0) for _ in range(3)] if last else None
        old = None if first else refs.pop(0)
        out, grad = refs[:2]
        more, scratch = refs[2:-3], refs[-3:]
        stencil = Stencil()
        pieces = [rl, r0, rh]

        def inverse(f, layer):
            return pieces[layer // WIDTH][FIELDS + f, layer % WIDTH]

        def emit(layer, x):
            for f in range(FIELDS):
                out[f, layer] = x[f]
                term = x[f] * u[f, layer]
                grad[f, layer] = term if first else old[f, layer] + term
                if not last:
                    r = src[f, layer]
                    if masses[f]:
                        r = r + (4.0 * x[f] - prev[f, layer])
                    for part in more:
                        part[f, layer] = r
                else:
                    z7, pack = more
                    z7[3 + f, layer] = x[f]
                    pack[0, f, layer] = x[f]
                    pack[1, f, layer] = prev[f, layer]
                    if masses[f]:
                        z7[f, layer] = x[f] - 0.25 * prev[f, layer]

        if last:
            for place in range(3):
                more[1][2 + place] = factors[place][2 * FIELDS :]
        else:
            for part in more:
                part[FIELDS : 2 * FIELDS] = inv[...]
        if first:
            more[0][2 * FIELDS :] = rl[2 * FIELDS :]
            more[1][2 * FIELDS :] = rh[2 * FIELDS :]
        solve(stencil, layers_of(pieces), inverse, 3 * WIDTH, scratch, emit)

    operands = [own, low, high, states, previous]
    operands += list(coarse) if last else [source, factor]
    operands += [] if first else [total]
    outs = [SLAB, SLAB]
    outs += [carry(7), (5,) + SLAB] if last else [carry(12)] * 2 if first else [carry(8)]
    return call(body, outs, *operands, layers=3 * WIDTH, flops=28 * 4 * 1024 * 20)


def carry(count):
    return (count, WIDTH, 8, 128)


def offsets_step(z_three, inv_five, pack, own_three, pair_odd):
    def body(*refs):
        (zl, zm, zh), iv, even, zo, (x0, x1) = refs[0:3], refs[3:8], refs[8], refs[9:12], refs[12:14]
        v, pairs = refs[14:16]
        scratch = refs[16:]
        z = [zl.at[0:3], zl.at[3:9], zm, zh.at[0:6], zh.at[6:9]]
        stencil = Stencil()

        def emit_odd(layer, q):
            slab, at = layer // WIDTH, layer % WIDTH
            for f in range(FIELDS):
                if masses[f]:
                    v[f, layer] = zo[slab][f, at] - 0.875 * q[f] + 0.125 * z[slab + 1][3 + f, at]
                if slab == 1:
                    pairs[0, 0, f, at] = x0[f, at] - q[f]
                    pairs[0, 1, f, at] = x1[f, at] - 0.5 * (q[f] + z[2][3 + f, at])

        def emit_even(layer, q):
            for f in range(FIELDS):
                pairs[1, 0, f, layer] = even[0, f, layer] - q[f]
                pairs[1, 1, f, layer] = even[1, f, layer] - 0.5 * (q[f] + x0[f, layer])

        inv_at = lambda f, layer: even[2 + layer // WIDTH, f, layer % WIDTH]
        solve(stencil, masses_only(z), layers_of(iv), 5 * WIDTH, scratch, emit_odd)
        solve(stencil, masses_only(zo), inv_at, 3 * WIDTH, scratch, emit_even)

    return call(
        body,
        [(3, 3 * WIDTH, 8, 128), (2, 2) + SLAB],
        *z_three, *inv_five, pack, *own_three, *pair_odd,
        layers=5 * WIDTH, flops=88 * 4 * 1024 * 20,
    )


def chip_step(turn, place, z_five, inv_five, pack, v_three, offsets, done, grad):
    with_done, with_grad, with_z = done is not None, grad is not None, z_five is not None

    def body(*refs):
        refs = list(refs)
        spot = refs.pop(0)
        z = [refs.pop(0) for _ in range(5)] if with_z else None
        iv = [refs.pop(0) for _ in range(5)]
        even, v, o = refs.pop(0), refs.pop(0), refs.pop(0)
        before = refs.pop(0) if with_done else None
        g = [refs.pop(0) for _ in range(2)] if with_grad else None
        z3, z6, z7, pairs = refs[:4]
        sums = refs[4] if with_grad else None
        middle, scratch = refs[-4], refs[-3:]
        if with_grad:
            sums[...] = g[0][...] + g[1][...]
        mine = spot[0] == turn

        @pl.when(jnp.logical_not(mine))
        def _():
            pairs[...] = before[...] if with_done else jnp.zeros_like(pairs)
            z3[...] = jnp.zeros_like(z3)
            z6[...] = jnp.zeros_like(z6)
            z7[...] = jnp.zeros_like(z7)

        @pl.when(mine)
        def _():
            stencil = Stencil()
            zero = jnp.zeros((8, 128), jnp.float32)

            def emit_odd(layer, q):
                slab, at = layer // WIDTH, layer % WIDTH
                for f in range(FIELDS):
                    own = slab == 1
                    c0 = z[slab + 1][3 + f, at] if with_z and (own or masses[f]) else zero
                    if masses[f]:
                        middle[f, layer] = 0.875 * q[f] - 0.125 * c0 + v[f, layer]
                    if own:
                        pairs[0, 0, f, at] = q[f] + o[0, 0, f, at]
                        pairs[0, 1, f, at] = 0.5 * (q[f] + c0) + o[0, 1, f, at]

            def emit_even(layer, q):
                for f in range(FIELDS):
                    c0 = q[f] + o[1, 0, f, layer]
                    c1 = 0.5 * (q[f] + pairs[0, 0, f, layer]) + o[1, 1, f, layer]
                    pairs[1, 0, f, layer] = c0
                    pairs[1, 1, f, layer] = c1
                    z7[3 + f, layer] = c0
                    if masses[f]:
                        carried = c0 - 0.25 * c1
                        z3[f, layer] = carried
                        z6[f, layer] = carried
                        z7[f, layer] = carried
                        z6[3 + f, layer] = c0

            if with_z:
                right = masses_only(z)
            else:
                right = lambda f, layer: zero if masses[f] else None
            middle_at = lambda f, layer: middle[f, layer] if masses[f] else None
            inv_at = lambda f, layer: even[2 + layer // WIDTH, f, layer % WIDTH]
            solve(stencil, right, layers_of(iv), 5 * WIDTH, scratch, emit_odd)
            solve(stencil, middle_at, inv_at, 3 * WIDTH, scratch, emit_even)

    spec = pl.BlockSpec(memory_space=pltpu.VMEM)
    operands = [place] + (list(z_five) if with_z else []) + list(inv_five) + [pack, v_three, offsets]
    operands += [done] if with_done else []
    operands += list(grad) if with_grad else []
    outs = [carry(3), carry(6), carry(7), (2, 2) + SLAB] + ([SLAB] if with_grad else [])
    return pl.pallas_call(
        body,
        in_specs=[pl.BlockSpec(memory_space=pltpu.SMEM)] + [spec] * (len(operands) - 1),
        out_specs=[spec] * len(outs),
        out_shape=[jax.ShapeDtypeStruct(shape, jnp.float32) for shape in outs],
        scratch_shapes=[vmem((3, 3 * WIDTH, 8, 128))] + [vmem((FIELDS, 5 * WIDTH, 8, 128))] * 3,
        compiler_params=pltpu.CompilerParams(vmem_limit_bytes=24 * 1024 * 1024),
        cost_estimate=pl.CostEstimate(flops=88 * 4 * 1024 * 20, bytes_accessed=1 << 20, transcendentals=0),
    )(*operands)


def routes(times, slabs, moved, chosen=None):
    pairs = []
    for k in range(times):
        for s in range(slabs):
            target = moved(k, s)
            if target is None or (chosen is not None and not chosen(k)):
                continue
            k2, s2 = target
            if 0 <= k2 < times and 0 <= s2 < slabs:
                pairs.append((k * slabs + s, k2 * slabs + s2))
    return pairs


def send(value, pairs):
    return lax.ppermute(value, AXES, pairs)


def program(times, slabs):
    chips = times // 2

    def shift(count):
        return routes(times, slabs, lambda k, s: (k, s + count))

    right_one, left_one = shift(1), shift(-1)
    earlier = routes(times, slabs, lambda k, s: (k - 1, s))
    even_to_odd = routes(times, slabs, lambda k, s: (k + 1, s), lambda k: k % 2 == 0)
    odd_to_even = routes(times, slabs, lambda k, s: (k - 1, s), lambda k: k % 2 == 1)
    reach = (2, 1, 0, -1, -2)
    relaxed_routes = [
        routes(times, slabs, lambda k, s, d=d: (k - 1, s + d), lambda k: k % 2 == 0) for d in (1, 0, -1)
    ]

    def hop_routes(hop):
        group = [h for h in range(1, chips) if (h - hop) % 4 == 0]
        senders = [2 * (chips - h) + 1 for h in group]
        return [
            routes(times, slabs, lambda k, s, d=d: (k - 2, s + d), lambda k: k in senders)
            for d in reach
        ]

    def on_device(forward_states, adjoint_source, source_gain, guess_pairs):
        states = forward_states.astype(jnp.float32)
        ahead = send(guess_pairs[0], earlier)
        inverses = [1.0 / make_diagonal(states[n], source_gain, fine_rate) for n in range(4)]
        coarse = 1.0 / make_diagonal(states[0], source_gain, coarse_rate)
        right = adjoint_source[3] + column(masses) * (4.0 * ahead[0] - ahead[1])
        up = down = jnp.concatenate([right, inverses[3], coarse])
        previous, total = ahead[0], None
        adjoints, exchanged = [None] * 4, []
        for n in (3, 2, 1, 0):
            low, high = send(up, right_one), send(down, left_one)
            exchanged.append((low, up, high))
            if n:
                rest = dict(source=adjoint_source[n - 1], factor=inverses[n - 1])
            else:
                rest = dict(coarse=exchanged[0])
            x, total, *more = fine_step(n, up, low, high, states[n], previous, total, **rest)
            adjoints[n] = previous = x
            up, down = more[0], more[-1]
        (low, own, high), (low_two, _, high_two) = exchanged[:2]
        inv_five = [part[2 * FIELDS :] for part in (low_two, low, own, high, high_two)]
        z7, pack = more
        total = time_step * total

        z_low, z_high = send(z7, right_one), send(z7, left_one)
        pack = send(pack, even_to_odd)
        payload = (
            jnp.concatenate([z_low[:3], z7[:6]]), z7, jnp.concatenate([z7[:6], z_high[:3]])
        )
        z_three = [send(part, path) for part, path in zip(payload, relaxed_routes)]
        v, offsets = offsets_step(
            z_three, inv_five, pack, (z_low, z7, z_high), (adjoints[0], adjoints[1])
        )

        place = (lax.axis_index("tm").astype(jnp.int32)).reshape(1)
        stages = []
        far = 1
        while far < chips:
            stages.append(
                routes(times, slabs, lambda k, s, d=far: (2 * ((k // 2) ^ d), s), lambda k: k % 2 == 0)
            )
            far *= 2
        stages = [odd_to_even] + stages
        z_five, done, grad, hop = None, None, total, 0
        while hop < chips or stages:
            added = None
            if hop and hop < chips:
                z_five = [send(part, path) for part, path in zip(payload, hop_routes(hop))]
            if hop and stages:
                arrived = sum(part[:1] if part.shape[0] < 4 else part[:4] for part in z_five)
                late = jnp.where(place[0] < 0, arrived, grad)
                added = (grad, send(late, stages.pop(0)))
            if hop < chips:
                z3, z6, z7, done, *sums = chip_step(
                    times - 1 - 2 * hop, place, z_five, inv_five, pack, v, offsets, done, added
                )
                payload = (z3, z6, z7, z6, z3)
                if sums:
                    grad = sums[0]
            elif added:
                grad = added[0] + added[1]
            hop += 1

        even = lax.axis_index("tm") % 2 == 0
        grad_odd = send(grad, even_to_odd)
        gradient = jnp.where(even, grad, grad_odd)
        done_even = send(done[1], odd_to_even)
        corrected = jnp.where(even, done_even, done[0])
        return corrected[None], gradient

    return on_device


def solution(mesh):
    placed = (
        P("tm", None, "space", None, None),
        P("tm", None, "space", None, None),
        P(None, "space", None, None),
        P("tm", None, None, "space", None, None),
    )
    return jax.shard_map(
        program(mesh.shape["tm"], mesh.shape["space"]),
        mesh=mesh,
        in_specs=placed,
        out_specs=(P("tm", None, None, "space", None, None), P(None, "space", None, None)),
        check_vma=False,
    )
```

```python
import jax
import jax.numpy as jnp
from jax import lax
from jax.experimental import pallas as pl
from jax.experimental.pallas import tpu as pltpu
from jax.sharding import PartitionSpec as P

SWEEPS = 4
FIELDS = 4
WIDTH = 4

diffusion = (2.4, 1.2, 0.6, 4.0)
fibre_weight = 128.0
reaction = (
    (-14.4, 7.2, -4.8, 2.4),
    (4.8, -19.2, 7.2, -4.8),
    (-7.2, 2.4, -12.0, 7.2),
    (4.8, -7.2, 2.4, -38.4),
)
self_rates = (-14.4, -19.2, -12.0, -38.4)
masses = (1.0, 1.0, 1.0, 0.0)
fine_rate = 3.0
coarse_rate = 0.75
time_step = 0.5
operator_scale = 0.0078125
state_weight = 0.1
gain_weight = 0.25

AXES = ("tm", "space")
SLAB = (FIELDS, WIDTH, 8, 128)


def column(values):
    return jnp.array(values, jnp.float32).reshape(4, 1, 1, 1)


def make_diagonal(state, source_gain, rate):
    stencil_total = (2.0 * fibre_weight + 4.0) * column(diffusion)
    spatial = operator_scale * (stencil_total - column(self_rates))
    return (
        rate * column(masses) + spatial + state_weight * state * state - gain_weight * source_gain
    )


class Stencil:
    def __init__(self):
        row = lax.broadcasted_iota(jnp.int32, (8, 128), 0)
        lane = lax.broadcasted_iota(jnp.int32, (8, 128), 1)
        self.first_row, self.last_row = row == 0, row == 7
        self.first_lane, self.last_lane = lane == 0, lane == 127

    def cross(self, cell):
        rows = jnp.where(self.first_row, 0.0, pltpu.roll(cell, 1, 0)) + jnp.where(
            self.last_row, 0.0, pltpu.roll(cell, 7, 0)
        )
        lanes = jnp.where(self.first_lane, 0.0, pltpu.roll(cell, 1, 1)) + jnp.where(
            self.last_lane, 0.0, pltpu.roll(cell, 127, 1)
        )
        return rows + lanes

    def sweep(self, below, here, above, start, inverse):
        fresh = []
        for f in range(FIELDS):
            spread = (operator_scale * fibre_weight * diffusion[f]) * (below[f] + above[f])
            spread = spread + (operator_scale * diffusion[f]) * self.cross(here[f])
            for g in range(FIELDS):
                if g != f:
                    spread = spread + (operator_scale * reaction[g][f]) * here[g]
            fresh.append(start[f] + inverse[f] * spread)
        return fresh


def solve(stencil, right, inverse, count, scratch, emit):
    base, ping, pong = scratch
    for layer in range(count):
        for f in range(FIELDS):
            value = right(f, layer)
            if value is None:
                base[f, layer] = jnp.zeros((8, 128), jnp.float32)
            else:
                base[f, layer] = value * inverse(f, layer)
    source = base
    for sweep in range(1, SWEEPS + 1):
        target = ping if sweep % 2 else pong
        for layer in range(sweep, count - sweep):
            below, here, above = (
                [source[f, layer + shift] for f in range(FIELDS)] for shift in (-1, 0, 1)
            )
            start = [base[f, layer] for f in range(FIELDS)]
            factor = [inverse(f, layer) for f in range(FIELDS)]
            fresh = stencil.sweep(below, here, above, start, factor)
            if sweep == SWEEPS:
                emit(layer - SWEEPS, fresh)
            else:
                for f in range(FIELDS):
                    target[f, layer] = fresh[f]
        source = target


def layers_of(pieces):
    return lambda f, layer: pieces[layer // WIDTH][f, layer % WIDTH]


def masses_only(pieces):
    read = layers_of(pieces)
    return lambda f, layer: read(f, layer) if masses[f] else None


def vmem(shape):
    return pltpu.VMEM(shape, jnp.float32)


def call(body, outs, *operands, smem=0, layers=0, flops=0):
    spec = pl.BlockSpec(memory_space=pltpu.VMEM)
    return pl.pallas_call(
        body,
        in_specs=[pl.BlockSpec(memory_space=pltpu.SMEM)] * smem + [spec] * (len(operands) - smem),
        out_specs=[spec] * len(outs),
        out_shape=[jax.ShapeDtypeStruct(shape, jnp.float32) for shape in outs],
        scratch_shapes=[vmem((FIELDS, layers, 8, 128))] * 3,
        compiler_params=pltpu.CompilerParams(vmem_limit_bytes=24 * 1024 * 1024),
        cost_estimate=pl.CostEstimate(flops=flops, bytes_accessed=1 << 20, transcendentals=0),
    )(*operands)


def fine_step(step, own, low, high, states, previous, total, source=None, factor=None, coarse=None):
    first, second, last = total is None, step == 2, step == 0

    def body(*refs):
        refs = list(refs)
        r0, rl, rh, u, prev = [refs.pop(0) for _ in range(5)]
        src, inv = (None, None) if last else [refs.pop(0) for _ in range(2)]
        factors = [refs.pop(0) for _ in range(4)][:3] if last else None
        old = None if first else refs.pop(0)
        out, grad = refs[:2]
        more, scratch = refs[2:-3], refs[-3:]
        stencil = Stencil()
        pieces = [rl, r0, rh]

        def inverse(f, layer):
            return pieces[layer // WIDTH][FIELDS + f, layer % WIDTH]

        def emit(layer, x):
            for f in range(FIELDS):
                out[f, layer] = x[f]
                term = x[f] * u[f, layer]
                grad[f, layer] = term if first else old[f, layer] + term
                if not last:
                    r = src[f, layer]
                    if masses[f]:
                        r = r + (4.0 * x[f] - prev[f, layer])
                    for part in more:
                        part[f, layer] = r
                else:
                    z7, pack = more
                    z7[3 + f, layer] = x[f]
                    pack[0, f, layer] = x[f]
                    pack[1, f, layer] = prev[f, layer]
                    if masses[f]:
                        z7[f, layer] = x[f] - 0.25 * prev[f, layer]

        if last:
            for place in range(3):
                more[1][2 + place] = factors[place][2 * FIELDS :]
        else:
            for part in more:
                part[FIELDS : 2 * FIELDS] = inv[...]
        if first:
            more[0][2 * FIELDS :] = rl[2 * FIELDS :]
            more[1][2 * FIELDS :] = rh[2 * FIELDS :]
        solve(stencil, layers_of(pieces), inverse, 3 * WIDTH, scratch, emit)

    operands = [own, low, high, states, previous]
    operands += list(coarse) if last else [source, factor]
    operands += [] if first else [total]
    outs = [SLAB, SLAB]
    outs += [carry(7), (5,) + SLAB] if last else [carry(12)] * 2 if first else [carry(8)]
    return call(body, outs, *operands, layers=3 * WIDTH, flops=28 * 4 * 1024 * 20)


def carry(count):
    return (count, WIDTH, 8, 128)


def offsets_step(pack, z_low, z_own, z_high, even_low, even_high, prior):
    def body(even, zl, z0, zh, el, eh, before, offset, ahead, own, *scratch):
        stencil = Stencil()
        for f in range(3):
            own[f] = even[0, f] - 0.25 * even[1, f]

        def emit_even(layer, q):
            for f in range(FIELDS):
                offset[0, f, layer] = even[0, f, layer] - q[f]
                offset[1, f, layer] = even[1, f, layer] - 0.5 * (q[f] + z0[3 + f, layer])

        def emit_before(layer, q):
            for f in range(FIELDS):
                ahead[f, layer] = q[f]

        inv_even = lambda f, layer: even[2 + layer // WIDTH, f, layer % WIDTH]
        inv_before = lambda f, layer: before[layer // WIDTH, f, layer % WIDTH]
        solve(stencil, masses_only([zl, z0, zh]), inv_even, 3 * WIDTH, scratch, emit_even)
        solve(stencil, masses_only([el, own, eh]), inv_before, 3 * WIDTH, scratch, emit_before)

    spec = pl.BlockSpec(memory_space=pltpu.VMEM)
    return pl.pallas_call(
        body,
        in_specs=[spec] * 7,
        out_specs=[spec] * 2,
        out_shape=[jax.ShapeDtypeStruct(shape, jnp.float32) for shape in ((2,) + SLAB, SLAB)],
        scratch_shapes=[vmem(carry(3))] + [vmem((FIELDS, 3 * WIDTH, 8, 128))] * 3,
        compiler_params=pltpu.CompilerParams(vmem_limit_bytes=24 * 1024 * 1024),
        cost_estimate=pl.CostEstimate(flops=56 * 4 * 1024 * 20, bytes_accessed=1 << 20, transcendentals=0),
    )(pack, z_low, z_own, z_high, even_low, even_high, prior)


def chip_step(turn, place, arrived, inv_five, pack, own_three, late, offset, ahead, done, grad):
    with_done, with_grad, with_z = done is not None, grad is not None, arrived is not None

    def body(*refs):
        refs = list(refs)
        spot = refs.pop(0)
        z = [refs.pop(0) for _ in range(5)] if with_z else None
        iv = [refs.pop(0) for _ in range(5)]
        even = refs.pop(0)
        zo = [refs.pop(0) for _ in range(3)]
        x1, o, qa = [refs.pop(0) for _ in range(3)]
        before = [refs.pop(0) for _ in range(2)] if with_done else None
        g = [refs.pop(0) for _ in range(2)] if with_grad else None
        z3, z6, z11, odd_pair, even_pair = refs[:5]
        sums = refs[5] if with_grad else None
        middle, scratch = refs[-4], refs[-3:]
        if with_grad:
            sums[...] = g[0][...] + g[1][...]
        mine = spot[0] == turn

        @pl.when(jnp.logical_not(mine))
        def _():
            odd_pair[...] = before[0][...] if with_done else jnp.zeros_like(odd_pair)
            even_pair[...] = before[1][...] if with_done else jnp.zeros_like(even_pair)
            z3[...] = jnp.zeros_like(z3)
            z6[...] = jnp.zeros_like(z6)
            z11[...] = jnp.zeros_like(z11)

        @pl.when(mine)
        def _():
            stencil = Stencil()
            zero = jnp.zeros((8, 128), jnp.float32)

            def emit_odd(layer, q):
                slab, at = layer // WIDTH, layer % WIDTH
                for f in range(FIELDS):
                    if slab == 1:
                        solved = z[2][3 + f, at] if with_z else zero
                        change = z[2][7 + f, at] if with_z else zero
                        c0 = q[f] + (zo[1][3 + f, at] - solved)
                        c1 = x1[f, at] + 0.5 * ((q[f] - solved) + change)
                        odd_pair[0, f, at] = c0
                        odd_pair[1, f, at] = c1
                        if masses[f]:
                            middle[f, layer] = c0 - 0.25 * c1
                    elif masses[f]:
                        y = z[slab + 1][3 + f, at] if with_z else zero
                        middle[f, layer] = 0.875 * q[f] + y + zo[slab][f, at]

            def emit_even(layer, q):
                for f in range(FIELDS):
                    c0 = q[f] + o[0, f, layer]
                    c1 = 0.5 * (q[f] + odd_pair[0, f, layer]) + o[1, f, layer]
                    change = c0 - even[0, f, layer]
                    even_pair[0, f, layer] = c0
                    even_pair[1, f, layer] = c1
                    z11[3 + f, layer] = qa[f, layer]
                    z11[7 + f, layer] = change
                    if masses[f]:
                        carried = c0 - 0.25 * c1
                        z3[f, layer] = carried
                        z6[f, layer] = carried
                        z11[f, layer] = carried
                        z6[3 + f, layer] = -0.875 * qa[f, layer] - 0.125 * change

            if with_z:
                right = masses_only(z)
            else:
                right = lambda f, layer: zero if masses[f] else None
            middle_at = lambda f, layer: middle[f, layer] if masses[f] else None
            inv_at = lambda f, layer: even[2 + layer // WIDTH, f, layer % WIDTH]
            solve(stencil, right, layers_of(iv), 5 * WIDTH, scratch, emit_odd)
            solve(stencil, middle_at, inv_at, 3 * WIDTH, scratch, emit_even)

    spec = pl.BlockSpec(memory_space=pltpu.VMEM)
    operands = [place] + (list(arrived) if with_z else []) + list(inv_five) + [pack]
    operands += list(own_three) + [late, offset, ahead]
    operands += list(done) if with_done else []
    operands += list(grad) if with_grad else []
    outs = [carry(3), carry(6), carry(11), (2,) + SLAB, (2,) + SLAB] + ([SLAB] if with_grad else [])
    return pl.pallas_call(
        body,
        in_specs=[pl.BlockSpec(memory_space=pltpu.SMEM)] + [spec] * (len(operands) - 1),
        out_specs=[spec] * len(outs),
        out_shape=[jax.ShapeDtypeStruct(shape, jnp.float32) for shape in outs],
        scratch_shapes=[vmem((3, 3 * WIDTH, 8, 128))] + [vmem((FIELDS, 5 * WIDTH, 8, 128))] * 3,
        compiler_params=pltpu.CompilerParams(vmem_limit_bytes=24 * 1024 * 1024),
        cost_estimate=pl.CostEstimate(flops=88 * 4 * 1024 * 20, bytes_accessed=1 << 20, transcendentals=0),
    )(*operands)


def routes(times, slabs, moved, chosen=None):
    pairs = []
    for k in range(times):
        for s in range(slabs):
            target = moved(k, s)
            if target is None or (chosen is not None and not chosen(k)):
                continue
            k2, s2 = target
            if 0 <= k2 < times and 0 <= s2 < slabs:
                pairs.append((k * slabs + s, k2 * slabs + s2))
    return pairs


def send(value, pairs):
    return lax.ppermute(value, AXES, pairs)


def program(times, slabs):
    chips = times // 2

    def shift(count):
        return routes(times, slabs, lambda k, s: (k, s + count))

    right_one, left_one = shift(1), shift(-1)
    earlier = routes(times, slabs, lambda k, s: (k - 1, s))
    even_to_odd = routes(times, slabs, lambda k, s: (k + 1, s), lambda k: k % 2 == 0)
    odd_to_even = routes(times, slabs, lambda k, s: (k - 1, s), lambda k: k % 2 == 1)
    reach = (2, 1, 0, -1, -2)
    odd, even = (lambda k: k % 2 == 1), (lambda k: k % 2 == 0)
    odd_right, odd_left = (routes(times, slabs, lambda k, s, d=d: (k, s + d), odd) for d in (1, -1))
    even_right, even_left = (
        routes(times, slabs, lambda k, s, d=d: (k + 1, s + d), even) for d in (1, -1)
    )
    later = routes(times, slabs, lambda k, s: (k + 2, s), odd)

    def hop_routes(hop):
        group = [h for h in range(1, chips) if (h - hop) % 4 == 0]
        senders = [2 * (chips - h) + 1 for h in group]
        return [
            routes(times, slabs, lambda k, s, d=d: (k - 2, s + d), lambda k: k in senders)
            for d in reach
        ]

    def on_device(forward_states, adjoint_source, source_gain, guess_pairs):
        states = forward_states.astype(jnp.float32)
        ahead = send(guess_pairs[0], earlier)
        inverses = [1.0 / make_diagonal(states[n], source_gain, fine_rate) for n in range(4)]
        coarse = 1.0 / make_diagonal(states[0], source_gain, coarse_rate)
        right = adjoint_source[3] + column(masses) * (4.0 * ahead[0] - ahead[1])
        up = down = jnp.concatenate([right, inverses[3], coarse])
        previous, total = ahead[0], None
        adjoints, exchanged = [None] * 4, []
        for n in (3, 2, 1, 0):
            low, high = send(up, right_one), send(down, left_one)
            exchanged.append((low, up, high))
            if n:
                rest = dict(source=adjoint_source[n - 1], factor=inverses[n - 1])
            else:
                far = [part[2 * FIELDS :] for part in exchanged[0]]
                prior = send(jnp.stack(far), later)
                rest = dict(coarse=(*exchanged[0], prior))
            x, total, *more = fine_step(n, up, low, high, states[n], previous, total, **rest)
            adjoints[n] = previous = x
            up, down = more[0], more[-1]
        (low, own, high), (low_two, _, high_two) = exchanged[:2]
        inv_five = [part[2 * FIELDS :] for part in (low_two, low, own, high, high_two)]
        z7, pack = more
        total = time_step * total

        z3 = z7[:3]
        z_low, z_high = send(z3, odd_right), send(z3, odd_left)
        even_low, even_high = send(z3, even_right), send(z3, even_left)
        pack = send(pack, even_to_odd)
        own_three = (z_low, z7, z_high)
        offset, before = offsets_step(pack, *own_three, even_low, even_high, prior)

        place = (lax.axis_index("tm").astype(jnp.int32)).reshape(1)
        stages = []
        far = 1
        while far < chips:
            stages.append(
                routes(times, slabs, lambda k, s, d=far: (2 * ((k // 2) ^ d), s), lambda k: k % 2 == 0)
            )
            far *= 2
        stages = [odd_to_even] + stages + [even_to_odd]
        is_even = lax.axis_index("tm") % 2 == 0
        arrived, done, grad, hop = None, None, total, 0
        while hop < chips or stages:
            added = None
            if hop and hop < chips:
                arrived = [send(part, path) for part, path in zip(payload, hop_routes(hop))]
            if hop and stages:
                mark = sum(part[:1] if part.shape[0] < 4 else part[:4] for part in arrived)
                received = send(jnp.where(place[0] < 0, mark, grad), stages.pop(0))
                added = (grad if stages else jnp.where(is_even, grad, 0.0), received)
            if hop < chips:
                z3, z6, z11, odd_pair, even_pair, *sums = chip_step(
                    times - 1 - 2 * hop, place, arrived, inv_five, pack, own_three, adjoints[1],
                    offset, before, done, added,
                )
                payload, done = (z3, z6, z11, z6, z3), (odd_pair, even_pair)
                if sums:
                    grad = sums[0]
            elif added:
                grad = added[0] + added[1]
            hop += 1

        corrected = jnp.where(is_even, send(done[1], odd_to_even), done[0])
        return corrected[None], grad

    return on_device


def solution(mesh):
    placed = (
        P("tm", None, "space", None, None),
        P("tm", None, "space", None, None),
        P(None, "space", None, None),
        P("tm", None, None, "space", None, None),
    )
    return jax.shard_map(
        program(mesh.shape["tm"], mesh.shape["space"]),
        mesh=mesh,
        in_specs=placed,
        out_specs=(P("tm", None, None, "space", None, None), P(None, "space", None, None)),
        check_vma=False,
    )
```

```python
import jax
import jax.numpy as jnp
from jax import lax
from jax.experimental import pallas as pl
from jax.experimental.pallas import tpu as pltpu
from jax.sharding import PartitionSpec as P

SWEEPS = 4
FIELDS = 4
WIDTH = 4

diffusion = (2.4, 1.2, 0.6, 4.0)
fibre_weight = 128.0
reaction = (
    (-14.4, 7.2, -4.8, 2.4),
    (4.8, -19.2, 7.2, -4.8),
    (-7.2, 2.4, -12.0, 7.2),
    (4.8, -7.2, 2.4, -38.4),
)
self_rates = (-14.4, -19.2, -12.0, -38.4)
masses = (1.0, 1.0, 1.0, 0.0)
fine_rate = 3.0
coarse_rate = 0.75
time_step = 0.5
operator_scale = 0.0078125
state_weight = 0.1
gain_weight = 0.25

AXES = ("tm", "space")
SLAB = (FIELDS, WIDTH, 8, 128)


def column(values):
    return jnp.array(values, jnp.float32).reshape(4, 1, 1, 1)


def make_diagonal(state, source_gain, rate):
    stencil_total = (2.0 * fibre_weight + 4.0) * column(diffusion)
    spatial = operator_scale * (stencil_total - column(self_rates))
    return (
        rate * column(masses) + spatial + state_weight * state * state - gain_weight * source_gain
    )


class Stencil:
    def __init__(self):
        row = lax.broadcasted_iota(jnp.int32, (8, 128), 0)
        lane = lax.broadcasted_iota(jnp.int32, (8, 128), 1)
        self.first_row, self.last_row = row == 0, row == 7
        self.first_lane, self.last_lane = lane == 0, lane == 127

    def cross(self, cell):
        rows = jnp.where(self.first_row, 0.0, pltpu.roll(cell, 1, 0)) + jnp.where(
            self.last_row, 0.0, pltpu.roll(cell, 7, 0)
        )
        lanes = jnp.where(self.first_lane, 0.0, pltpu.roll(cell, 1, 1)) + jnp.where(
            self.last_lane, 0.0, pltpu.roll(cell, 127, 1)
        )
        return rows + lanes

    def sweep(self, below, here, above, start, inverse):
        fresh = []
        for f in range(FIELDS):
            spread = (operator_scale * fibre_weight * diffusion[f]) * (below[f] + above[f])
            spread = spread + (operator_scale * diffusion[f]) * self.cross(here[f])
            for g in range(FIELDS):
                if g != f:
                    spread = spread + (operator_scale * reaction[g][f]) * here[g]
            fresh.append(start[f] + inverse[f] * spread)
        return fresh


def solve(stencil, right, inverse, lowest, slabs, count, scratch, emit):
    base, ping, pong = scratch
    cut = [lax.rem(lowest + (slabs + at), slabs) == 0 for at in range(count)]
    count = count * WIDTH
    for layer in range(count):
        for f in range(FIELDS):
            value = right(f, layer)
            if value is None:
                base[f, layer] = jnp.zeros((8, 128), jnp.float32)
            else:
                base[f, layer] = value * inverse(f, layer)
    source = base
    for sweep in range(1, SWEEPS + 1):
        target = ping if sweep % 2 else pong
        for layer in range(sweep, count - sweep):
            below, here, above = (
                [source[f, layer + shift] for f in range(FIELDS)] for shift in (-1, 0, 1)
            )
            if layer % WIDTH == 0:
                below = [jnp.where(cut[layer // WIDTH], 0.0, cell) for cell in below]
            if layer % WIDTH == WIDTH - 1:
                above = [jnp.where(cut[layer // WIDTH + 1], 0.0, cell) for cell in above]
            start = [base[f, layer] for f in range(FIELDS)]
            factor = [inverse(f, layer) for f in range(FIELDS)]
            fresh = stencil.sweep(below, here, above, start, factor)
            if sweep == SWEEPS:
                emit(layer - SWEEPS, fresh)
            else:
                for f in range(FIELDS):
                    target[f, layer] = fresh[f]
        source = target


def layers_of(pieces):
    return lambda f, layer: pieces[layer // WIDTH][f, layer % WIDTH]


def masses_only(pieces):
    read = layers_of(pieces)
    return lambda f, layer: read(f, layer) if masses[f] else None


def vmem(shape):
    return pltpu.VMEM(shape, jnp.float32)


def call(body, outs, *operands, smem=0, layers=0, flops=0):
    spec = pl.BlockSpec(memory_space=pltpu.VMEM)
    return pl.pallas_call(
        body,
        in_specs=[pl.BlockSpec(memory_space=pltpu.SMEM)] * smem + [spec] * (len(operands) - smem),
        out_specs=[spec] * len(outs),
        out_shape=[jax.ShapeDtypeStruct(shape, jnp.float32) for shape in outs],
        scratch_shapes=[vmem((FIELDS, layers, 8, 128))] * 3,
        compiler_params=pltpu.CompilerParams(vmem_limit_bytes=24 * 1024 * 1024),
        cost_estimate=pl.CostEstimate(flops=flops, bytes_accessed=1 << 20, transcendentals=0),
    )(*operands)


def fine_step(step, place, slabs, own, low, high, states, previous, total, source=None, factor=None, coarse=None):
    first, second, last = total is None, step == 2, step == 0

    def body(*refs):
        refs = list(refs)
        spot = refs.pop(0)
        r0, rl, rh, u, prev = [refs.pop(0) for _ in range(5)]
        src, inv = (None, None) if last else [refs.pop(0) for _ in range(2)]
        factors = [refs.pop(0) for _ in range(5)][:4] if last else None
        old = None if first else refs.pop(0)
        out = None if last else refs.pop(0)
        grad, more, scratch = refs[0], refs[1:-3], refs[-3:]
        stencil = Stencil()
        pieces = [rl, r0, rh]

        def inverse(f, layer):
            return pieces[layer // WIDTH][FIELDS + f, layer % WIDTH]

        def emit(layer, x):
            for f in range(FIELDS):
                if not last:
                    out[f, layer] = x[f]
                term = x[f] * u[f, layer]
                grad[f, layer] = term if first else old[f, layer] + term
                if not last:
                    r = src[f, layer]
                    if masses[f]:
                        r = r + (4.0 * x[f] - prev[f, layer])
                    for part in more:
                        part[f, layer] = r
                else:
                    z7, pack = more
                    z7[3 + f, layer] = x[f]
                    pack[0, f, layer] = x[f]
                    pack[1, f, layer] = prev[f, layer]
                    if masses[f]:
                        z7[f, layer] = x[f] - 0.25 * prev[f, layer]

        if last:
            for place in range(4):
                more[1][2 + place] = factors[place][2 * FIELDS :]
        else:
            for part in more:
                part[FIELDS : 2 * FIELDS] = inv[...]
        if first:
            more[0][2 * FIELDS :] = rl[2 * FIELDS :]
        if first or second:
            more[1][2 * FIELDS :] = rh[2 * FIELDS :]
        solve(stencil, layers_of(pieces), inverse, spot[1] - 1, slabs, 3, scratch, emit)

    operands = [place, own, low, high, states, previous]
    operands += list(coarse) if last else [source, factor]
    operands += [] if first else [total]
    outs = [SLAB, carry(7), (6,) + SLAB] if last else [SLAB, SLAB]
    outs += [] if last else [carry(12)] * 2 if first else [carry(8), carry(12)] if second else [carry(8)]
    return call(body, outs, *operands, smem=1, layers=3 * WIDTH, flops=28 * 4 * 1024 * 20)


def carry(count):
    return (count, WIDTH, 8, 128)


def offsets_step(place, slabs, even, four, prior):
    def body(spot, pack, z0, z1, z2, z3, before, own, ahead, *scratch):
        stencil = Stencil()
        z = [z0, z1, z2, z3]

        def emit_to(target):
            def emit(layer, q):
                for f in range(FIELDS):
                    target[f, layer] = q[f]

            return emit

        inv_own = lambda f, layer: pack[2 + layer // WIDTH, f, layer % WIDTH]
        inv_before = lambda f, layer: before[layer // WIDTH, f, layer % WIDTH]
        z_own = [part.at[0:3] for part in z]
        z_even = [part.at[3:6] for part in z]
        lowest = spot[1] - 1
        solve(stencil, masses_only(z_own), inv_own, lowest, slabs, 4, scratch, emit_to(own))
        solve(stencil, masses_only(z_even), inv_before, lowest, slabs, 4, scratch, emit_to(ahead))

    wide = (FIELDS, 2 * WIDTH, 8, 128)
    operands = (place, even, *four, prior)
    return call(body, [wide, wide], *operands, smem=1, layers=4 * WIDTH, flops=88 * 4 * 1024 * 20)


def chip_step(turn, place, slabs, arrived, inv_six, even, four, pair, own, ahead, done, grad):
    with_done, with_grad, with_z = done is not None, grad is not None, arrived is not None

    def body(*refs):
        refs = list(refs)
        take = lambda count: [refs.pop(0) for _ in range(count)]
        (spot,) = take(1)
        za, zb, zc = take(3) if with_z else [None] * 3
        iv = take(6)
        (pack,) = take(1)
        zr = take(4)
        z7, x1, qe, qa = take(4)
        before = take(2) if with_done else None
        g = take(2) if with_grad else None
        up, down, straight, odd_pair, even_pair = take(5)
        sums = take(1)[0] if with_grad else None
        middle, moved, *scratch = refs
        if with_grad:
            sums[...] = g[0][...] + g[1][...]
        mine = spot[0] == turn

        @pl.when(jnp.logical_not(mine))
        def _():
            odd_pair[...] = before[0][...] if with_done else jnp.zeros_like(odd_pair)
            even_pair[...] = before[1][...] if with_done else jnp.zeros_like(even_pair)
            for part in (up, down, straight):
                part[...] = jnp.zeros_like(part)

        @pl.when(mine)
        def _():
            stencil = Stencil()
            zero = jnp.zeros((8, 128), jnp.float32)
            read = lambda ref, f, at: ref[f, at] if with_z else zero

            def emit_odd(layer, q):
                slab, at = layer // WIDTH, layer % WIDTH
                for f in range(FIELDS):
                    if slab == 1:
                        solved, change = read(zb, 6 + f, at), read(zb, 13 + f, at)
                        c0 = q[f] + (z7[3 + f, at] - solved)
                        c1 = x1[f, at] + 0.5 * ((q[f] - solved) + change)
                        odd_pair[0, f, at] = c0
                        odd_pair[1, f, at] = c1
                        if masses[f]:
                            middle[f, layer] = c0 - 0.25 * c1
                    elif masses[f] and slab == 2:
                        solved, change = read(zb, 10 + f, at), read(zb, 17 + f, at)
                        moved[f, at] = q[f] - solved
                        middle[f, layer] = zr[2][f, at] + 0.875 * (q[f] - solved) - 0.125 * change
                    elif masses[f]:
                        y = read(za if slab == 0 else zc, 6 + f, at)
                        middle[f, layer] = 0.875 * q[f] + y + zr[slab][f, at]

            def emit_even(layer, q):
                slab, at = layer // WIDTH, layer % WIDTH
                for f in range(FIELDS):
                    if slab == 0:
                        c0 = q[f] + (pack[0, f, at] - qe[f, layer])
                        c1 = 0.5 * (q[f] + odd_pair[0, f, at]) + (
                            pack[1, f, at] - 0.5 * (qe[f, layer] + z7[3 + f, at])
                        )
                        even_pair[0, f, at] = c0
                        even_pair[1, f, at] = c1
                        change, z = c0 - pack[0, f, at], c0 - 0.25 * c1
                        straight[6 + f, at] = qa[f, layer]
                        straight[13 + f, at] = change
                    elif masses[f]:
                        change = q[f] - qe[f, layer]
                        z = zr[2][3 + f, at] + 0.875 * change - 0.125 * moved[f, at]
                        straight[10 + f, at] = qa[f, layer]
                        straight[17 + f, at] = change
                    if masses[f]:
                        for part in (up, down, straight):
                            part[3 * slab + f, at] = z
                        y = -0.875 * qa[f, layer] - 0.125 * change
                        (up if slab else down)[6 + f, at] = y

            if with_z:
                z = [za.at[0:3], za.at[3:6], zb.at[0:3], zb.at[3:6], zc.at[0:3], zc.at[3:6]]
                right = masses_only(z)
            else:
                right = lambda f, layer: zero if masses[f] else None
            middle_at = lambda f, layer: middle[f, layer] if masses[f] else None
            inv_at = lambda f, layer: pack[2 + layer // WIDTH, f, layer % WIDTH]
            solve(stencil, right, layers_of(iv), spot[1] - 2, slabs, 6, scratch, emit_odd)
            solve(stencil, middle_at, inv_at, spot[1] - 1, slabs, 4, scratch, emit_even)

    spec = pl.BlockSpec(memory_space=pltpu.VMEM)
    operands = [place] + (list(arrived) if with_z else []) + list(inv_six) + [even]
    operands += list(four) + list(pair) + [own, ahead]
    operands += list(done) if with_done else []
    operands += list(grad) if with_grad else []
    outs = [carry(9), carry(9), carry(20), (2,) + SLAB, (2,) + SLAB] + ([SLAB] if with_grad else [])
    return pl.pallas_call(
        body,
        in_specs=[pl.BlockSpec(memory_space=pltpu.SMEM)] + [spec] * (len(operands) - 1),
        out_specs=[spec] * len(outs),
        out_shape=[jax.ShapeDtypeStruct(shape, jnp.float32) for shape in outs],
        scratch_shapes=[vmem((3, 4 * WIDTH, 8, 128)), vmem(carry(3))]
        + [vmem((FIELDS, 6 * WIDTH, 8, 128))] * 3,
        compiler_params=pltpu.CompilerParams(vmem_limit_bytes=24 * 1024 * 1024),
        cost_estimate=pl.CostEstimate(flops=120 * 4 * 1024 * 20, bytes_accessed=1 << 20, transcendentals=0),
    )(*operands)


def routes(times, slabs, moved, chosen=None):
    pairs = []
    for k in range(times):
        for s in range(slabs):
            target = moved(k, s)
            if target is None or (chosen is not None and not chosen(k)):
                continue
            k2, s2 = target
            if 0 <= k2 < times:
                pairs.append((k * slabs + s, k2 * slabs + s2 % slabs))
    return pairs


def send(value, pairs):
    return lax.ppermute(value, AXES, pairs)


def program(times, slabs):
    chips = times // 2

    def shift(count):
        return routes(times, slabs, lambda k, s: (k, s + count))

    right_one, left_one = shift(1), shift(-1)
    earlier = routes(times, slabs, lambda k, s: (k - 1, s))
    even_to_odd = routes(times, slabs, lambda k, s: (k + 1, s), lambda k: k % 2 == 0)
    odd_to_even = routes(times, slabs, lambda k, s: (k - 1, s), lambda k: k % 2 == 1)
    odd, even = (lambda k: k % 2 == 1), (lambda k: k % 2 == 0)
    odd_right, odd_left, odd_left_two = (
        routes(times, slabs, lambda k, s, d=d: (k, s + d), odd) for d in (1, -1, -2)
    )
    later = routes(times, slabs, lambda k, s: (k + 2, s), odd)

    def hop_routes(hop):
        sender = 2 * (chips - hop) + 1
        return [
            routes(times, slabs, lambda k, s, d=d: (k - 2, s + d), lambda k: k == sender)
            for d in (2, 0, -2)
        ]

    def on_device(forward_states, adjoint_source, source_gain, guess_pairs):
        place = jnp.stack([lax.axis_index("tm"), lax.axis_index("space")]).astype(jnp.int32)
        states = forward_states.astype(jnp.float32)
        ahead = send(guess_pairs[0], earlier)
        inverses = [1.0 / make_diagonal(states[n], source_gain, fine_rate) for n in range(4)]
        coarse = 1.0 / make_diagonal(states[0], source_gain, coarse_rate)
        right = adjoint_source[3] + column(masses) * (4.0 * ahead[0] - ahead[1])
        up = down = jnp.concatenate([right, inverses[3], coarse])
        previous, total = ahead[0], None
        exchanged = []
        for n in (3, 2, 1, 0):
            low, high = send(up, right_one), send(down, left_one)
            exchanged.append((low, up, high))
            if n == 0:
                far = [part[2 * FIELDS :] for part in (*exchanged[0], exchanged[1][2])]
                prior = send(jnp.stack(far), later)
                rest = dict(coarse=(*exchanged[0], exchanged[1][2], prior))
            else:
                rest = dict(source=adjoint_source[n - 1], factor=inverses[n - 1])
            step = fine_step(n, place, slabs, up, low, high, states[n], previous, total, **rest)
            if n:
                previous, total, up, *more = step
                down = more[0] if more else up
        total, z7, even_pack = step
        total = time_step * total
        (low, own, high), (low_two, _, high_two), (_, _, high_three) = exchanged[:3]
        inv_six = [part[2 * FIELDS :] for part in (low_two, low, own, high, high_two, high_three)]

        even_pack = send(even_pack, even_to_odd)
        both = jnp.concatenate([z7[:3], even_pack[0, :3] - 0.25 * even_pack[1, :3]])
        four = [send(both, odd_right), both, send(both, odd_left), send(both, odd_left_two)]
        solved, ahead_solved = offsets_step(place, slabs, even_pack, four, prior)

        stages = []
        far = 1
        while far < chips:
            stages.append(
                routes(times, slabs, lambda k, s, d=far: (2 * ((k // 2) ^ d), s), lambda k: k % 2 == 0)
            )
            far *= 2
        stages = [odd_to_even] + stages + [even_to_odd]
        is_even = lax.axis_index("tm") % 2 == 0
        arrived, done, grad, hop = None, None, total, 0
        while hop < chips or stages:
            added = None
            if hop and hop < chips:
                arrived = [send(part, path) for part, path in zip(payload, hop_routes(hop))]
            if hop and stages:
                received = send(grad, stages.pop(0))
                added = (grad if stages else jnp.where(is_even, grad, 0.0), received)
            if hop < chips:
                up, down, straight, odd_pair, even_pair, *sums = chip_step(
                    times - 1 - 2 * hop, place, slabs, arrived, inv_six, even_pack, four, (z7, previous),
                    solved, ahead_solved, done, added,
                )
                payload, done = (up, straight, down), (odd_pair, even_pair)
                if sums:
                    grad = sums[0]
            elif added:
                grad = added[0] + added[1]
            hop += 1

        corrected = jnp.where(is_even, send(done[1], odd_to_even), done[0])
        return corrected[None], grad

    return on_device


def solution(mesh):
    placed = (
        P("tm", None, "space", None, None),
        P("tm", None, "space", None, None),
        P(None, "space", None, None),
        P("tm", None, None, "space", None, None),
    )
    return jax.shard_map(
        program(mesh.shape["tm"], mesh.shape["space"]),
        mesh=mesh,
        in_specs=placed,
        out_specs=(P("tm", None, None, "space", None, None), P(None, "space", None, None)),
        check_vma=False,
    )
```

```python
import jax
import jax.numpy as jnp
from jax import lax
from jax.experimental import pallas as pl
from jax.experimental.pallas import tpu as pltpu
from jax.sharding import PartitionSpec as P

SWEEPS = 4
FIELDS = 4
WIDTH = 4

diffusion = (2.4, 1.2, 0.6, 4.0)
fibre_weight = 128.0
reaction = (
    (-14.4, 7.2, -4.8, 2.4),
    (4.8, -19.2, 7.2, -4.8),
    (-7.2, 2.4, -12.0, 7.2),
    (4.8, -7.2, 2.4, -38.4),
)
self_rates = (-14.4, -19.2, -12.0, -38.4)
masses = (1.0, 1.0, 1.0, 0.0)
fine_rate = 3.0
coarse_rate = 0.75
time_step = 0.5
operator_scale = 0.0078125
state_weight = 0.1
gain_weight = 0.25

AXES = ("tm", "space")
SLAB = (FIELDS, WIDTH, 8, 128)


def column(values):
    return jnp.array(values, jnp.float32).reshape(4, 1, 1, 1)


def make_diagonal(state, source_gain, rate):
    stencil_total = (2.0 * fibre_weight + 4.0) * column(diffusion)
    spatial = operator_scale * (stencil_total - column(self_rates))
    return (
        rate * column(masses) + spatial + state_weight * state * state - gain_weight * source_gain
    )


class Stencil:
    def __init__(self):
        row = lax.broadcasted_iota(jnp.int32, (8, 128), 0)
        lane = lax.broadcasted_iota(jnp.int32, (8, 128), 1)
        self.first_row, self.last_row = row == 0, row == 7
        self.first_lane, self.last_lane = lane == 0, lane == 127

    def cross(self, cell):
        rows = jnp.where(self.first_row, 0.0, pltpu.roll(cell, 1, 0)) + jnp.where(
            self.last_row, 0.0, pltpu.roll(cell, 7, 0)
        )
        lanes = jnp.where(self.first_lane, 0.0, pltpu.roll(cell, 1, 1)) + jnp.where(
            self.last_lane, 0.0, pltpu.roll(cell, 127, 1)
        )
        return rows + lanes

    def sweep(self, below, here, above, start, inverse):
        fresh = []
        for f in range(FIELDS):
            spread = (operator_scale * fibre_weight * diffusion[f]) * (below[f] + above[f])
            spread = spread + (operator_scale * diffusion[f]) * self.cross(here[f])
            for g in range(FIELDS):
                if g != f:
                    spread = spread + (operator_scale * reaction[g][f]) * here[g]
            fresh.append(start[f] + inverse[f] * spread)
        return fresh


def solve(stencil, right, inverse, count, scratch, emit):
    base, ping, pong = scratch
    for layer in range(count):
        for f in range(FIELDS):
            value = right(f, layer)
            if value is None:
                base[f, layer] = jnp.zeros((8, 128), jnp.float32)
            else:
                base[f, layer] = value * inverse(f, layer)
    source = base
    for sweep in range(1, SWEEPS + 1):
        target = ping if sweep % 2 else pong
        for layer in range(sweep, count - sweep):
            below, here, above = (
                [source[f, layer + shift] for f in range(FIELDS)] for shift in (-1, 0, 1)
            )
            start = [base[f, layer] for f in range(FIELDS)]
            factor = [inverse(f, layer) for f in range(FIELDS)]
            fresh = stencil.sweep(below, here, above, start, factor)
            if sweep == SWEEPS:
                emit(layer - SWEEPS, fresh)
            else:
                for f in range(FIELDS):
                    target[f, layer] = fresh[f]
        source = target


def layers_of(pieces):
    return lambda f, layer: pieces[layer // WIDTH][f, layer % WIDTH]


def masses_only(pieces):
    read = layers_of(pieces)
    return lambda f, layer: read(f, layer) if masses[f] else None


def vmem(shape):
    return pltpu.VMEM(shape, jnp.float32)


def call(body, outs, *operands, smem=0, layers=0, flops=0):
    spec = pl.BlockSpec(memory_space=pltpu.VMEM)
    return pl.pallas_call(
        body,
        in_specs=[pl.BlockSpec(memory_space=pltpu.SMEM)] * smem + [spec] * (len(operands) - smem),
        out_specs=[spec] * len(outs),
        out_shape=[jax.ShapeDtypeStruct(shape, jnp.float32) for shape in outs],
        scratch_shapes=[vmem((FIELDS, layers, 8, 128))] * 3,
        compiler_params=pltpu.CompilerParams(vmem_limit_bytes=24 * 1024 * 1024),
        cost_estimate=pl.CostEstimate(flops=flops, bytes_accessed=1 << 20, transcendentals=0),
    )(*operands)


def fine_step(step, own, low, high, states, previous, total, source=None, factor=None, coarse=None):
    first, second, last = total is None, step == 2, step == 0

    def body(*refs):
        refs = list(refs)
        r0, rl, rh, u, prev = [refs.pop(0) for _ in range(5)]
        src, inv = (None, None) if last else [refs.pop(0) for _ in range(2)]
        factors = [refs.pop(0) for _ in range(4)][:3] if last else None
        old = None if first else refs.pop(0)
        out = None if last else refs.pop(0)
        grad, more, scratch = refs[0], refs[1:-3], refs[-3:]
        stencil = Stencil()
        pieces = [rl, r0, rh]

        def inverse(f, layer):
            return pieces[layer // WIDTH][FIELDS + f, layer % WIDTH]

        def emit(layer, x):
            for f in range(FIELDS):
                if not last:
                    out[f, layer] = x[f]
                term = x[f] * u[f, layer]
                so_far = term if first else old[f, layer] + term
                if last:
                    so_far = time_step * so_far
                    more[1][5, f, layer] = so_far
                grad[f, layer] = so_far
                if not last:
                    r = src[f, layer]
                    if masses[f]:
                        r = r + (4.0 * x[f] - prev[f, layer])
                    for part in more:
                        part[f, layer] = r
                else:
                    z7, pack = more
                    z7[3 + f, layer] = x[f]
                    pack[0, f, layer] = x[f]
                    pack[1, f, layer] = prev[f, layer]
                    if masses[f]:
                        z7[f, layer] = x[f] - 0.25 * prev[f, layer]

        if last:
            for place in range(3):
                more[1][2 + place] = factors[place][2 * FIELDS :]
        else:
            for part in more:
                part[FIELDS : 2 * FIELDS] = inv[...]
        if first:
            more[0][2 * FIELDS :] = rl[2 * FIELDS :]
            more[1][2 * FIELDS :] = rh[2 * FIELDS :]
        solve(stencil, layers_of(pieces), inverse, 3 * WIDTH, scratch, emit)

    operands = [own, low, high, states, previous]
    operands += list(coarse) if last else [source, factor]
    operands += [] if first else [total]
    outs = [SLAB, carry(7), (6,) + SLAB] if last else [SLAB, SLAB]
    outs += [] if last else [carry(12)] * 2 if first else [carry(8)]
    return call(body, outs, *operands, layers=3 * WIDTH, flops=28 * 4 * 1024 * 20)


def carry(count):
    return (count, WIDTH, 8, 128)


def offsets_step(pack, z_low, z_own, z_high, x0, prior):
    def body(even, zl, z0, zh, z7, before, offset, ahead, *scratch):
        stencil = Stencil()

        def emit_even(layer, q):
            for f in range(FIELDS):
                offset[0, f, layer] = even[0, f, layer] - q[f]
                offset[1, f, layer] = even[1, f, layer] - 0.5 * (q[f] + z7[3 + f, layer])

        def emit_before(layer, q):
            for f in range(FIELDS):
                ahead[f, layer] = q[f]

        inv_even = lambda f, layer: even[2 + layer // WIDTH, f, layer % WIDTH]
        inv_before = lambda f, layer: before[layer // WIDTH, f, layer % WIDTH]
        solve(stencil, masses_only([zl, z0, zh]), inv_even, 3 * WIDTH, scratch, emit_even)
        z_even = [part.at[3:6] for part in (zl, z0, zh)]
        solve(stencil, masses_only(z_even), inv_before, 3 * WIDTH, scratch, emit_before)

    operands = (pack, z_low, z_own, z_high, x0, prior)
    return call(body, [(2,) + SLAB, SLAB], *operands, layers=3 * WIDTH, flops=56 * 4 * 1024 * 20)


def chip_step(turn, place, arrived, inv_five, pack, own_three, pair, offset, ahead, done, grad):
    with_done, with_grad, with_z = done is not None, grad is not None, arrived is not None

    def body(*refs):
        refs = list(refs)
        spot = refs.pop(0)
        z = [refs.pop(0) for _ in range(5)] if with_z else None
        iv = [refs.pop(0) for _ in range(5)]
        even = refs.pop(0)
        zo = [refs.pop(0) for _ in range(3)]
        z7, x1, o, qa = [refs.pop(0) for _ in range(4)]
        before = [refs.pop(0) for _ in range(2)] if with_done else None
        g = [refs.pop(0) for _ in range(2)] if with_grad else None
        z3, z6, z11, odd_pair, even_pair = refs[:5]
        middle, scratch = refs[-4], refs[-3:]
        if with_grad:
            refs[5][...] = g[0][...] + g[1][...]
        mine = spot[0] == turn

        @pl.when(jnp.logical_not(mine))
        def _():
            odd_pair[...] = before[0][...] if with_done else jnp.zeros_like(odd_pair)
            even_pair[...] = before[1][...] if with_done else jnp.zeros_like(even_pair)
            z3[...] = jnp.zeros_like(z3)
            z6[...] = jnp.zeros_like(z6)
            z11[...] = jnp.zeros_like(z11)

        @pl.when(mine)
        def _():
            stencil = Stencil()
            zero = jnp.zeros((8, 128), jnp.float32)

            def emit_odd(layer, q):
                slab, at = layer // WIDTH, layer % WIDTH
                for f in range(FIELDS):
                    if slab == 1:
                        solved = z[2][3 + f, at] if with_z else zero
                        change = z[2][7 + f, at] if with_z else zero
                        c0 = q[f] + (z7[3 + f, at] - solved)
                        c1 = x1[f, at] + 0.5 * ((q[f] - solved) + change)
                        odd_pair[0, f, at] = c0
                        odd_pair[1, f, at] = c1
                        if masses[f]:
                            middle[f, layer] = c0 - 0.25 * c1
                    elif masses[f]:
                        y = z[slab + 1][3 + f, at] if with_z else zero
                        middle[f, layer] = 0.875 * q[f] + y + zo[slab][f, at]

            def emit_even(layer, q):
                for f in range(FIELDS):
                    c0 = q[f] + o[0, f, layer]
                    c1 = 0.5 * (q[f] + odd_pair[0, f, layer]) + o[1, f, layer]
                    change = c0 - even[0, f, layer]
                    even_pair[0, f, layer] = c0
                    even_pair[1, f, layer] = c1
                    z11[3 + f, layer] = qa[f, layer]
                    z11[7 + f, layer] = change
                    if masses[f]:
                        carried = c0 - 0.25 * c1
                        z3[f, layer] = carried
                        z6[f, layer] = carried
                        z11[f, layer] = carried
                        z6[3 + f, layer] = -0.875 * qa[f, layer] - 0.125 * change

            if with_z:
                right = masses_only(z)
            else:
                right = lambda f, layer: zero if masses[f] else None
            middle_at = lambda f, layer: middle[f, layer] if masses[f] else None
            inv_at = lambda f, layer: even[2 + layer // WIDTH, f, layer % WIDTH]
            solve(stencil, right, layers_of(iv), 5 * WIDTH, scratch, emit_odd)
            solve(stencil, middle_at, inv_at, 3 * WIDTH, scratch, emit_even)

    spec = pl.BlockSpec(memory_space=pltpu.VMEM)
    operands = [place] + (list(arrived) if with_z else []) + list(inv_five) + [pack]
    operands += list(own_three) + list(pair) + [offset, ahead]
    operands += list(done) if with_done else []
    operands += list(grad) if with_grad else []
    outs = [carry(3), carry(6), carry(11), (2,) + SLAB, (2,) + SLAB]
    outs += [SLAB] if with_grad else []
    return pl.pallas_call(
        body,
        in_specs=[pl.BlockSpec(memory_space=pltpu.SMEM)] + [spec] * (len(operands) - 1),
        out_specs=[spec] * len(outs),
        out_shape=[jax.ShapeDtypeStruct(shape, jnp.float32) for shape in outs],
        scratch_shapes=[vmem((3, 3 * WIDTH, 8, 128))] + [vmem((FIELDS, 5 * WIDTH, 8, 128))] * 3,
        compiler_params=pltpu.CompilerParams(vmem_limit_bytes=24 * 1024 * 1024),
        cost_estimate=pl.CostEstimate(flops=88 * 4 * 1024 * 20, bytes_accessed=1 << 20, transcendentals=0),
    )(*operands)


def routes(times, slabs, moved, chosen=None):
    pairs = []
    for k in range(times):
        for s in range(slabs):
            target = moved(k, s)
            if target is None or (chosen is not None and not chosen(k)):
                continue
            k2, s2 = target
            if 0 <= k2 < times and 0 <= s2 < slabs:
                pairs.append((k * slabs + s, k2 * slabs + s2))
    return pairs


def send(value, pairs):
    return lax.ppermute(value, AXES, pairs)


def program(times, slabs):
    chips = times // 2

    def shift(count):
        return routes(times, slabs, lambda k, s: (k, s + count))

    right_one, left_one = shift(1), shift(-1)
    earlier = routes(times, slabs, lambda k, s: (k - 1, s))
    even_to_odd = routes(times, slabs, lambda k, s: (k + 1, s), lambda k: k % 2 == 0)
    swap = routes(times, slabs, lambda k, s: (k ^ 1, s))
    odd_to_even = routes(times, slabs, lambda k, s: (k - 1, s), lambda k: k % 2 == 1)
    reach = (2, 1, 0, -1, -2)
    odd, even = (lambda k: k % 2 == 1), (lambda k: k % 2 == 0)
    odd_right, odd_left = (routes(times, slabs, lambda k, s, d=d: (k, s + d), odd) for d in (1, -1))
    later = routes(times, slabs, lambda k, s: (k + 2, s), odd)

    def hop_routes(hop):
        group = [h for h in range(1, chips) if (h - hop) % 4 == 0]
        senders = [2 * (chips - h) + 1 for h in group]
        return [
            routes(times, slabs, lambda k, s, d=d: (k - 2, s + d), lambda k: k in senders)
            for d in reach
        ]

    def on_device(forward_states, adjoint_source, source_gain, guess_pairs):
        states = forward_states.astype(jnp.float32)
        ahead = send(guess_pairs[0], earlier)
        inverses = [1.0 / make_diagonal(states[n], source_gain, fine_rate) for n in range(4)]
        coarse = 1.0 / make_diagonal(states[0], source_gain, coarse_rate)
        right = adjoint_source[3] + column(masses) * (4.0 * ahead[0] - ahead[1])
        up = down = jnp.concatenate([right, inverses[3], coarse])
        previous, total = ahead[0], None
        exchanged = []
        for n in (3, 2, 1, 0):
            low, high = send(up, right_one), send(down, left_one)
            exchanged.append((low, up, high))
            if n:
                rest = dict(source=adjoint_source[n - 1], factor=inverses[n - 1])
            else:
                far = [part[2 * FIELDS :] for part in exchanged[0]]
                prior = send(jnp.stack(far), later)
                rest = dict(coarse=(*exchanged[0], prior))
            step = fine_step(n, up, low, high, states[n], previous, total, **rest)
            if n:
                previous, total, up, *more = step
                down = more[0] if more else up
        (low, own, high), (low_two, _, high_two) = exchanged[:2]
        inv_five = [part[2 * FIELDS :] for part in (low_two, low, own, high, high_two)]
        total, z7, pack = step

        pack = send(pack, swap)
        grad = total + pack[5]
        both = jnp.concatenate([z7[:3], pack[0, :3] - 0.25 * pack[1, :3]])
        own_three = (send(both, odd_right), both, send(both, odd_left))
        offset, before = offsets_step(pack, *own_three, z7, prior)

        place = (lax.axis_index("tm").astype(jnp.int32)).reshape(1)
        is_even = lax.axis_index("tm") % 2 == 0
        stages = []
        far = 1
        while far < chips:
            stages.append(routes(times, slabs, lambda k, s, d=far: (2 * ((k // 2) ^ d), s), even))
            far *= 2
        stages.append(even_to_odd)
        arrived, done = None, None
        for hop in range(max(chips, len(stages) + 1)):
            added = None
            if hop and hop < chips:
                arrived = [send(part, path) for part, path in zip(payload, hop_routes(hop))]
            if hop and stages:
                mark = sum(part[:1] if part.shape[0] < 4 else part[:4] for part in arrived)
                received = send(jnp.where(place[0] < 0, mark, grad), stages.pop(0))
                added = (grad if stages else jnp.where(is_even, grad, 0.0), received)
            if hop < chips:
                z3, z6, z11, odd_pair, even_pair, *sums = chip_step(
                    times - 1 - 2 * hop, place, arrived, inv_five, pack, own_three, (z7, previous),
                    offset, before, done, added,
                )
                payload, done = (z3, z6, z11, z6, z3), (odd_pair, even_pair)
                if sums:
                    grad = sums[0]
            elif added:
                grad = added[0] + added[1]

        corrected = jnp.where(is_even, send(done[1], odd_to_even), done[0])
        return corrected[None], grad

    return on_device


def solution(mesh):
    placed = (
        P("tm", None, "space", None, None),
        P("tm", None, "space", None, None),
        P(None, "space", None, None),
        P("tm", None, None, "space", None, None),
    )
    return jax.shard_map(
        program(mesh.shape["tm"], mesh.shape["space"]),
        mesh=mesh,
        in_specs=placed,
        out_specs=(P("tm", None, None, "space", None, None), P(None, "space", None, None)),
        check_vma=False,
    )
```

```python
import jax
import jax.numpy as jnp
from jax import lax
from jax.experimental import pallas as pl
from jax.experimental.pallas import tpu as pltpu
from jax.sharding import PartitionSpec as P

SWEEPS = 4
FIELDS = 4
WIDTH = 4

diffusion = (2.4, 1.2, 0.6, 4.0)
fibre_weight = 128.0
reaction = (
    (-14.4, 7.2, -4.8, 2.4),
    (4.8, -19.2, 7.2, -4.8),
    (-7.2, 2.4, -12.0, 7.2),
    (4.8, -7.2, 2.4, -38.4),
)
self_rates = (-14.4, -19.2, -12.0, -38.4)
masses = (1.0, 1.0, 1.0, 0.0)
fine_rate = 3.0
coarse_rate = 0.75
time_step = 0.5
operator_scale = 0.0078125
state_weight = 0.1
gain_weight = 0.25

AXES = ("tm", "space")
SLAB = (FIELDS, WIDTH, 8, 128)


def column(values):
    return jnp.array(values, jnp.float32).reshape(4, 1, 1, 1)


def make_diagonal(state, source_gain, rate):
    stencil_total = (2.0 * fibre_weight + 4.0) * column(diffusion)
    spatial = operator_scale * (stencil_total - column(self_rates))
    return (
        rate * column(masses) + spatial + state_weight * state * state - gain_weight * source_gain
    )


class Stencil:
    def __init__(self):
        row = lax.broadcasted_iota(jnp.int32, (8, 128), 0)
        lane = lax.broadcasted_iota(jnp.int32, (8, 128), 1)
        self.first_row, self.last_row = row == 0, row == 7
        self.first_lane, self.last_lane = lane == 0, lane == 127

    def cross(self, cell):
        rows = jnp.where(self.first_row, 0.0, pltpu.roll(cell, 1, 0)) + jnp.where(
            self.last_row, 0.0, pltpu.roll(cell, 7, 0)
        )
        lanes = jnp.where(self.first_lane, 0.0, pltpu.roll(cell, 1, 1)) + jnp.where(
            self.last_lane, 0.0, pltpu.roll(cell, 127, 1)
        )
        return rows + lanes

    def sweep(self, below, here, above, start, inverse):
        fresh = []
        for f in range(FIELDS):
            spread = (operator_scale * fibre_weight * diffusion[f]) * (below[f] + above[f])
            spread = spread + (operator_scale * diffusion[f]) * self.cross(here[f])
            for g in range(FIELDS):
                if g != f:
                    spread = spread + (operator_scale * reaction[g][f]) * here[g]
            fresh.append(start[f] + inverse[f] * spread)
        return fresh


def solve(stencil, right, inverse, count, scratch, emit):
    base, ping, pong = scratch
    for layer in range(count):
        for f in range(FIELDS):
            value = right(f, layer)
            if value is None:
                base[f, layer] = jnp.zeros((8, 128), jnp.float32)
            else:
                base[f, layer] = value * inverse(f, layer)
    source = base
    for sweep in range(1, SWEEPS + 1):
        target = ping if sweep % 2 else pong
        for layer in range(sweep, count - sweep):
            below, here, above = (
                [source[f, layer + shift] for f in range(FIELDS)] for shift in (-1, 0, 1)
            )
            start = [base[f, layer] for f in range(FIELDS)]
            factor = [inverse(f, layer) for f in range(FIELDS)]
            fresh = stencil.sweep(below, here, above, start, factor)
            if sweep == SWEEPS:
                emit(layer - SWEEPS, fresh)
            else:
                for f in range(FIELDS):
                    target[f, layer] = fresh[f]
        source = target


def layers_of(pieces):
    return lambda f, layer: pieces[layer // WIDTH][f, layer % WIDTH]


def masses_only(pieces):
    read = layers_of(pieces)
    return lambda f, layer: read(f, layer) if masses[f] else None


def vmem(shape):
    return pltpu.VMEM(shape, jnp.float32)


def call(body, outs, *operands, smem=0, layers=0, flops=0):
    spec = pl.BlockSpec(memory_space=pltpu.VMEM)
    return pl.pallas_call(
        body,
        in_specs=[pl.BlockSpec(memory_space=pltpu.SMEM)] * smem + [spec] * (len(operands) - smem),
        out_specs=[spec] * len(outs),
        out_shape=[jax.ShapeDtypeStruct(shape, jnp.float32) for shape in outs],
        scratch_shapes=[vmem((FIELDS, layers, 8, 128))] * 3,
        compiler_params=pltpu.CompilerParams(vmem_limit_bytes=24 * 1024 * 1024),
        cost_estimate=pl.CostEstimate(flops=flops, bytes_accessed=1 << 20, transcendentals=0),
    )(*operands)


def fine_step(step, own, low, high, states, previous, total, source=None, factor=None, coarse=None):
    first, second, last = total is None, step == 2, step == 0

    def body(*refs):
        refs = list(refs)
        r0, rl, rh, u, prev = [refs.pop(0) for _ in range(5)]
        src, inv = (None, None) if last else [refs.pop(0) for _ in range(2)]
        factors = [refs.pop(0) for _ in range(3)] if last else None
        old = None if first else refs.pop(0)
        out = None if last else refs.pop(0)
        grad, more, scratch = refs[0], refs[1:-3], refs[-3:]
        stencil = Stencil()
        pieces = [rl, r0, rh]

        def inverse(f, layer):
            return pieces[layer // WIDTH][FIELDS + f, layer % WIDTH]

        def emit(layer, x):
            for f in range(FIELDS):
                if not last:
                    out[f, layer] = x[f]
                term = x[f] * u[f, layer]
                so_far = term if first else old[f, layer] + term
                if last:
                    so_far = time_step * so_far
                    more[1][5, f, layer] = so_far
                grad[f, layer] = so_far
                if not last:
                    r = src[f, layer]
                    if masses[f]:
                        r = r + (4.0 * x[f] - prev[f, layer])
                    for part in more:
                        part[f, layer] = r
                else:
                    z7, pack = more
                    z7[3 + f, layer] = x[f]
                    pack[0, f, layer] = x[f]
                    pack[1, f, layer] = prev[f, layer]
                    if masses[f]:
                        z7[f, layer] = x[f] - 0.25 * prev[f, layer]

        if last:
            for place in range(3):
                more[1][2 + place] = factors[place][2 * FIELDS :]
        else:
            for part in more:
                part[FIELDS : 2 * FIELDS] = inv[...]
        if first:
            more[0][2 * FIELDS :] = rl[2 * FIELDS :]
            more[1][2 * FIELDS :] = rh[2 * FIELDS :]
        solve(stencil, layers_of(pieces), inverse, 3 * WIDTH, scratch, emit)

    operands = [own, low, high, states, previous]
    operands += list(coarse) if last else [source, factor]
    operands += [] if first else [total]
    outs = [SLAB, carry(7), (6,) + SLAB] if last else [SLAB, SLAB]
    outs += [] if last else [carry(12)] * 2 if first else [carry(8)]
    return call(body, outs, *operands, layers=3 * WIDTH, flops=28 * 4 * 1024 * 20)


def carry(count):
    return (count, WIDTH, 8, 128)


def offsets_step(pack, z_low, z_own, z_high, x0, prior):
    def body(even, zl, z0, zh, z7, before, offset, ahead, *scratch):
        stencil = Stencil()

        def emit_even(layer, q):
            for f in range(FIELDS):
                offset[0, f, layer] = even[0, f, layer] - q[f]
                offset[1, f, layer] = even[1, f, layer] - 0.5 * (q[f] + z7[3 + f, layer])

        def emit_before(layer, q):
            for f in range(FIELDS):
                ahead[f, layer] = q[f]

        inv_even = lambda f, layer: even[2 + layer // WIDTH, f, layer % WIDTH]
        inv_before = lambda f, layer: before[layer // WIDTH, f, layer % WIDTH]
        solve(stencil, masses_only([zl, z0, zh]), inv_even, 3 * WIDTH, scratch, emit_even)
        z_even = [part.at[3:6] for part in (zl, z0, zh)]
        solve(stencil, masses_only(z_even), inv_before, 3 * WIDTH, scratch, emit_before)

    operands = (pack, z_low, z_own, z_high, x0, prior)
    return call(body, [(2,) + SLAB, SLAB], *operands, layers=3 * WIDTH, flops=56 * 4 * 1024 * 20)


def chip_step(turn, place, arrived, inv_five, pack, own_three, pair, offset, ahead, solved, done, grad):
    with_done, with_grad, with_z = done is not None, grad is not None, arrived is not None
    final = turn == 1

    def body(*refs):
        refs = list(refs)
        spot = refs.pop(0)
        z = [refs.pop(0) for _ in range(5)] if with_z else None
        iv = [refs.pop(0) for _ in range(5)]
        even = refs.pop(0)
        zo = [refs.pop(0) for _ in range(3)]
        z7, x1, o, qa = [refs.pop(0) for _ in range(4)]
        qs = refs.pop(0) if with_z else None
        before = [refs.pop(0) for _ in range(2)] if with_done else None
        g = [refs.pop(0) for _ in range(2)] if with_grad else None
        odd_pair, even_pair = refs.pop(0), refs.pop(0)
        sums = refs.pop(0) if with_grad else None
        z3, z6, z7_out = [None] * 3 if final else refs[:3]
        middle, scratch = refs[-4], refs[-3:]
        if with_grad:
            sums[...] = g[0][...] + g[1][...]
        mine = spot[0] == turn

        @pl.when(jnp.logical_not(mine))
        def _():
            odd_pair[...] = before[0][...] if with_done else jnp.zeros_like(odd_pair)
            even_pair[...] = before[1][...] if with_done else jnp.zeros_like(even_pair)
            for part in () if final else (z3, z6, z7_out):
                part[...] = jnp.zeros_like(part)

        @pl.when(mine)
        def _():
            stencil = Stencil()
            zero = jnp.zeros((8, 128), jnp.float32)

            def emit_odd(layer, q):
                slab, at = layer // WIDTH, layer % WIDTH
                for f in range(FIELDS):
                    if slab == 1:
                        before_q = qs[f, at] if with_z else zero
                        change = z[2][3 + f, at] if with_z else zero
                        c0 = q[f] + (z7[3 + f, at] - before_q)
                        c1 = x1[f, at] + 0.5 * ((q[f] - before_q) + change)
                        odd_pair[0, f, at] = c0
                        odd_pair[1, f, at] = c1
                        if masses[f]:
                            middle[f, layer] = c0 - 0.25 * c1
                    elif masses[f]:
                        y = z[slab + 1][3 + f, at] if with_z else zero
                        middle[f, layer] = 0.875 * q[f] + y + zo[slab][f, at]

            def emit_even(layer, q):
                for f in range(FIELDS):
                    c0 = q[f] + o[0, f, layer]
                    c1 = 0.5 * (q[f] + odd_pair[0, f, layer]) + o[1, f, layer]
                    change = c0 - even[0, f, layer]
                    even_pair[0, f, layer] = c0
                    even_pair[1, f, layer] = c1
                    if final:
                        continue
                    z7_out[3 + f, layer] = change
                    if masses[f]:
                        carried = c0 - 0.25 * c1
                        z3[f, layer] = carried
                        z6[f, layer] = carried
                        z7_out[f, layer] = carried
                        z6[3 + f, layer] = -0.875 * qa[f, layer] - 0.125 * change

            if with_z:
                right = masses_only(z)
            else:
                right = lambda f, layer: zero if masses[f] else None
            middle_at = lambda f, layer: middle[f, layer] if masses[f] else None
            inv_at = lambda f, layer: even[2 + layer // WIDTH, f, layer % WIDTH]
            solve(stencil, right, layers_of(iv), 5 * WIDTH, scratch, emit_odd)
            solve(stencil, middle_at, inv_at, 3 * WIDTH, scratch, emit_even)

    spec = pl.BlockSpec(memory_space=pltpu.VMEM)
    operands = [place] + (list(arrived) if with_z else []) + list(inv_five) + [pack]
    operands += list(own_three) + list(pair) + [offset, ahead]
    operands += [solved] if with_z else []
    operands += list(done) if with_done else []
    operands += list(grad) if with_grad else []
    outs = [(2,) + SLAB, (2,) + SLAB] + ([SLAB] if with_grad else [])
    outs += [] if final else [carry(3), carry(6), carry(7)]
    return pl.pallas_call(
        body,
        in_specs=[pl.BlockSpec(memory_space=pltpu.SMEM)] + [spec] * (len(operands) - 1),
        out_specs=[spec] * len(outs),
        out_shape=[jax.ShapeDtypeStruct(shape, jnp.float32) for shape in outs],
        scratch_shapes=[vmem((3, 3 * WIDTH, 8, 128))] + [vmem((FIELDS, 5 * WIDTH, 8, 128))] * 3,
        compiler_params=pltpu.CompilerParams(vmem_limit_bytes=24 * 1024 * 1024),
        cost_estimate=pl.CostEstimate(flops=88 * 4 * 1024 * 20, bytes_accessed=1 << 20, transcendentals=0),
    )(*operands)


def routes(times, slabs, moved, chosen=None):
    pairs = []
    for k in range(times):
        for s in range(slabs):
            target = moved(k, s)
            if target is None or (chosen is not None and not chosen(k)):
                continue
            k2, s2 = target
            if 0 <= k2 < times and 0 <= s2 < slabs:
                pairs.append((k * slabs + s, k2 * slabs + s2))
    return pairs


def send(value, pairs):
    return lax.ppermute(value, AXES, pairs)


def program(times, slabs):
    chips = times // 2

    def shift(count):
        return routes(times, slabs, lambda k, s: (k, s + count))

    right_one, left_one = shift(1), shift(-1)
    earlier = routes(times, slabs, lambda k, s: (k - 1, s))
    even_to_odd = routes(times, slabs, lambda k, s: (k + 1, s), lambda k: k % 2 == 0)
    swap = routes(times, slabs, lambda k, s: (k ^ 1, s))
    odd_to_even = routes(times, slabs, lambda k, s: (k - 1, s), lambda k: k % 2 == 1)
    reach = (2, 1, 0, -1, -2)
    odd, even = (lambda k: k % 2 == 1), (lambda k: k % 2 == 0)
    odd_right, odd_left = (routes(times, slabs, lambda k, s, d=d: (k, s + d), odd) for d in (1, -1))
    later = routes(times, slabs, lambda k, s: (k + 2, s), odd)
    sooner = routes(times, slabs, lambda k, s: (k - 2, s), odd)

    def hop_routes(hop):
        group = [h for h in range(1, chips) if (h - hop) % 4 == 0]
        senders = [2 * (chips - h) + 1 for h in group]
        return [
            routes(times, slabs, lambda k, s, d=d: (k - 2, s + d), lambda k: k in senders)
            for d in reach
        ]

    def on_device(forward_states, adjoint_source, source_gain, guess_pairs):
        states = forward_states.astype(jnp.float32)
        ahead = send(guess_pairs[0], earlier)
        inverses = [1.0 / make_diagonal(states[n], source_gain, fine_rate) for n in range(4)]
        coarse = 1.0 / make_diagonal(states[0], source_gain, coarse_rate)
        right = adjoint_source[3] + column(masses) * (4.0 * ahead[0] - ahead[1])
        up = down = jnp.concatenate([right, inverses[3], coarse])
        previous, total = ahead[0], None
        exchanged = []
        for n in (3, 2, 1, 0):
            low, high = send(up, right_one), send(down, left_one)
            exchanged.append((low, up, high))
            if n:
                rest = dict(source=adjoint_source[n - 1], factor=inverses[n - 1])
            else:
                rest = dict(coarse=exchanged[0])
            step = fine_step(n, up, low, high, states[n], previous, total, **rest)
            if n:
                previous, total, up, *more = step
                down = more[0] if more else up
        (low, own, high), (low_two, _, high_two) = exchanged[:2]
        inv_five = [part[2 * FIELDS :] for part in (low_two, low, own, high, high_two)]
        total, z7, pack = step

        prior = send(jnp.stack([part[2 * FIELDS :] for part in (low, own, high)]), later)
        pack = send(pack, swap)
        grad = total + pack[5]
        both = jnp.concatenate([z7[:3], pack[0, :3] - 0.25 * pack[1, :3]])
        own_three = (send(both, odd_right), both, send(both, odd_left))
        offset, before = offsets_step(pack, *own_three, z7, prior)
        solved = send(before, sooner)

        place = (lax.axis_index("tm").astype(jnp.int32)).reshape(1)
        is_even = lax.axis_index("tm") % 2 == 0
        stages = []
        far = 1
        while far < chips:
            stages.append(routes(times, slabs, lambda k, s, d=far: (2 * ((k // 2) ^ d), s), even))
            far *= 2
        stages.append(even_to_odd)
        arrived, done = None, None
        for hop in range(max(chips, len(stages) + 1)):
            added = None
            if hop and hop < chips:
                arrived = [send(part, path) for part, path in zip(payload, hop_routes(hop))]
            if hop and stages:
                mark = sum(part[:1] if part.shape[0] < 4 else part[:4] for part in arrived)
                received = send(jnp.where(place[0] < 0, mark, grad), stages.pop(0))
                added = (grad if stages else jnp.where(is_even, grad, 0.0), received)
            if hop < chips:
                odd_pair, even_pair, *more = chip_step(
                    times - 1 - 2 * hop, place, arrived, inv_five, pack, own_three, (z7, previous),
                    offset, before, solved if hop else None, done, added,
                )
                if added:
                    grad = more.pop(0)
                if hop < chips - 1:
                    z3, z6, z7_out = more
                    if not hop:
                        z3, z6, z7_out = (jnp.where(place[0] < 0, solved[:1], p) for p in more)
                    payload = (z3, z6, z7_out, z6, z3)
                done = (odd_pair, even_pair)
            elif added:
                grad = added[0] + added[1]

        corrected = jnp.where(is_even, send(done[1], odd_to_even), done[0])
        return corrected[None], grad

    return on_device


def solution(mesh):
    placed = (
        P("tm", None, "space", None, None),
        P("tm", None, "space", None, None),
        P(None, "space", None, None),
        P("tm", None, None, "space", None, None),
    )
    return jax.shard_map(
        program(mesh.shape["tm"], mesh.shape["space"]),
        mesh=mesh,
        in_specs=placed,
        out_specs=(P("tm", None, None, "space", None, None), P(None, "space", None, None)),
        check_vma=False,
    )
```

```python
import jax
import jax.numpy as jnp
from jax import lax
from jax.experimental import pallas as pl
from jax.experimental.pallas import tpu as pltpu
from jax.sharding import PartitionSpec as P

SWEEPS = 4
FIELDS = 4
WIDTH = 4

diffusion = (2.4, 1.2, 0.6, 4.0)
fibre_weight = 128.0
reaction = (
    (-14.4, 7.2, -4.8, 2.4),
    (4.8, -19.2, 7.2, -4.8),
    (-7.2, 2.4, -12.0, 7.2),
    (4.8, -7.2, 2.4, -38.4),
)
self_rates = (-14.4, -19.2, -12.0, -38.4)
masses = (1.0, 1.0, 1.0, 0.0)
fine_rate = 3.0
coarse_rate = 0.75
time_step = 0.5
operator_scale = 0.0078125
state_weight = 0.1
gain_weight = 0.25

AXES = ("tm", "space")
SLAB = (FIELDS, WIDTH, 8, 128)


def column(values):
    return jnp.array(values, jnp.float32).reshape(4, 1, 1, 1)


def make_diagonal(state, source_gain, rate):
    stencil_total = (2.0 * fibre_weight + 4.0) * column(diffusion)
    spatial = operator_scale * (stencil_total - column(self_rates))
    return (
        rate * column(masses) + spatial + state_weight * state * state - gain_weight * source_gain
    )


class Stencil:
    def __init__(self):
        row = lax.broadcasted_iota(jnp.int32, (8, 128), 0)
        lane = lax.broadcasted_iota(jnp.int32, (8, 128), 1)
        self.first_row, self.last_row = row == 0, row == 7
        self.first_lane, self.last_lane = lane == 0, lane == 127

    def cross(self, cell):
        rows = jnp.where(self.first_row, 0.0, pltpu.roll(cell, 1, 0)) + jnp.where(
            self.last_row, 0.0, pltpu.roll(cell, 7, 0)
        )
        lanes = jnp.where(self.first_lane, 0.0, pltpu.roll(cell, 1, 1)) + jnp.where(
            self.last_lane, 0.0, pltpu.roll(cell, 127, 1)
        )
        return rows + lanes

    def sweep(self, below, here, above, start, inverse):
        fresh = []
        for f in range(FIELDS):
            spread = (operator_scale * fibre_weight * diffusion[f]) * (below[f] + above[f])
            spread = spread + (operator_scale * diffusion[f]) * self.cross(here[f])
            for g in range(FIELDS):
                if g != f:
                    spread = spread + (operator_scale * reaction[g][f]) * here[g]
            fresh.append(start[f] + inverse[f] * spread)
        return fresh


def solve(stencil, right, inverse, count, scratch, emit):
    base, ping, pong = scratch
    for layer in range(count):
        for f in range(FIELDS):
            value = right(f, layer)
            if value is None:
                base[f, layer] = jnp.zeros((8, 128), jnp.float32)
            else:
                base[f, layer] = value * inverse(f, layer)
    source = base
    for sweep in range(1, SWEEPS + 1):
        target = ping if sweep % 2 else pong
        for layer in range(sweep, count - sweep):
            below, here, above = (
                [source[f, layer + shift] for f in range(FIELDS)] for shift in (-1, 0, 1)
            )
            start = [base[f, layer] for f in range(FIELDS)]
            factor = [inverse(f, layer) for f in range(FIELDS)]
            fresh = stencil.sweep(below, here, above, start, factor)
            if sweep == SWEEPS:
                emit(layer - SWEEPS, fresh)
            else:
                for f in range(FIELDS):
                    target[f, layer] = fresh[f]
        source = target


def layers_of(pieces):
    return lambda f, layer: pieces[layer // WIDTH][f, layer % WIDTH]


def masses_only(pieces):
    read = layers_of(pieces)
    return lambda f, layer: read(f, layer) if masses[f] else None


def vmem(shape):
    return pltpu.VMEM(shape, jnp.float32)


def call(body, outs, *operands, smem=0, layers=0, flops=0):
    spec = pl.BlockSpec(memory_space=pltpu.VMEM)
    return pl.pallas_call(
        body,
        in_specs=[pl.BlockSpec(memory_space=pltpu.SMEM)] * smem + [spec] * (len(operands) - smem),
        out_specs=[spec] * len(outs),
        out_shape=[jax.ShapeDtypeStruct(shape, jnp.float32) for shape in outs],
        scratch_shapes=[vmem((FIELDS, layers, 8, 128))] * 3,
        compiler_params=pltpu.CompilerParams(vmem_limit_bytes=24 * 1024 * 1024),
        cost_estimate=pl.CostEstimate(flops=flops, bytes_accessed=1 << 20, transcendentals=0),
    )(*operands)


def fine_step(step, own, low, high, states, previous, total, source=None, factor=None, coarse=None):
    first, second, last = total is None, step == 2, step == 0

    def body(*refs):
        refs = list(refs)
        r0, rl, rh, u, prev = [refs.pop(0) for _ in range(5)]
        src, inv = (None, None) if last else [refs.pop(0) for _ in range(2)]
        factors = [refs.pop(0) for _ in range(3)] if last else None
        old = None if first else refs.pop(0)
        out = None if last else refs.pop(0)
        grad, more, scratch = refs[0], refs[1:-3], refs[-3:]
        stencil = Stencil()
        pieces = [rl, r0, rh]

        def inverse(f, layer):
            return pieces[layer // WIDTH][FIELDS + f, layer % WIDTH]

        def emit(layer, x):
            for f in range(FIELDS):
                if not last:
                    out[f, layer] = x[f]
                term = x[f] * u[f, layer]
                so_far = term if first else old[f, layer] + term
                if last:
                    so_far = time_step * so_far
                    more[1][5, f, layer] = so_far
                grad[f, layer] = so_far
                if not last:
                    r = src[f, layer]
                    if masses[f]:
                        r = r + (4.0 * x[f] - prev[f, layer])
                    for part in more:
                        part[f, layer] = r
                else:
                    z7, pack = more
                    z7[3 + f, layer] = x[f]
                    pack[0, f, layer] = x[f]
                    pack[1, f, layer] = prev[f, layer]
                    if masses[f]:
                        z7[f, layer] = x[f] - 0.25 * prev[f, layer]

        if last:
            for place in range(3):
                more[1][2 + place] = factors[place][2 * FIELDS :]
        else:
            for part in more:
                part[FIELDS : 2 * FIELDS] = inv[...]
        if first:
            more[0][2 * FIELDS :] = rl[2 * FIELDS :]
            more[1][2 * FIELDS :] = rh[2 * FIELDS :]
        solve(stencil, layers_of(pieces), inverse, 3 * WIDTH, scratch, emit)

    operands = [own, low, high, states, previous]
    operands += list(coarse) if last else [source, factor]
    operands += [] if first else [total]
    outs = [SLAB, carry(7), (6,) + SLAB] if last else [SLAB, SLAB]
    outs += [] if last else [carry(12)] * 2 if first else [carry(8)]
    return call(body, outs, *operands, layers=3 * WIDTH, flops=28 * 4 * 1024 * 20)


def carry(count):
    return (count, WIDTH, 8, 128)


def offsets_step(pack, z_low, z_own, z_high, x0, prior):
    def body(even, zl, z0, zh, z7, before, offset, ahead, *scratch):
        stencil = Stencil()

        def emit_even(layer, q):
            for f in range(FIELDS):
                offset[0, f, layer] = even[0, f, layer] - q[f]
                offset[1, f, layer] = even[1, f, layer] - 0.5 * (q[f] + z7[3 + f, layer])

        def emit_before(layer, q):
            for f in range(FIELDS):
                ahead[f, layer] = q[f]

        inv_even = lambda f, layer: even[2 + layer // WIDTH, f, layer % WIDTH]
        inv_before = lambda f, layer: before[layer // WIDTH, f, layer % WIDTH]
        solve(stencil, masses_only([zl, z0, zh]), inv_even, 3 * WIDTH, scratch, emit_even)
        z_even = [part.at[3:6] for part in (zl, z0, zh)]
        solve(stencil, masses_only(z_even), inv_before, 3 * WIDTH, scratch, emit_before)

    operands = (pack, z_low, z_own, z_high, x0, prior)
    return call(body, [(2,) + SLAB, SLAB], *operands, layers=3 * WIDTH, flops=56 * 4 * 1024 * 20)


def chip_step(turn, place, arrived, inv_five, pack, own_three, pair, offset, ahead, solved, done, grad, mark):
    with_done, with_grad, with_z = done is not None, grad is not None, arrived is not None
    final = turn == 1

    def body(*refs):
        refs = list(refs)
        spot = refs.pop(0)
        z = [refs.pop(0) for _ in range(5)] if with_z else None
        iv = [refs.pop(0) for _ in range(5)]
        even = refs.pop(0)
        zo = [refs.pop(0) for _ in range(3)]
        z7, x1, o, qa = [refs.pop(0) for _ in range(4)]
        qs = refs.pop(0) if with_z else None
        before = [refs.pop(0) for _ in range(2)] if with_done else None
        g = [refs.pop(0) for _ in range(2)] if with_grad else None
        if mark is not None:
            refs.pop(0)
        odd_pair, even_pair = refs.pop(0), refs.pop(0)
        sums = refs.pop(0) if with_grad else None
        z3, z6, z7_out = [None] * 3 if final else refs[:3]
        middle, scratch = refs[-4], refs[-3:]
        if with_grad:
            sums[...] = g[0][...] + g[1][...]
        mine = spot[0] == turn

        @pl.when(jnp.logical_not(mine))
        def _():
            odd_pair[...] = before[0][...] if with_done else jnp.zeros_like(odd_pair)
            even_pair[...] = before[1][...] if with_done else jnp.zeros_like(even_pair)
            for part in () if final else (z3, z6, z7_out):
                part[...] = jnp.zeros_like(part)

        @pl.when(mine)
        def _():
            stencil = Stencil()
            zero = jnp.zeros((8, 128), jnp.float32)

            def emit_odd(layer, q):
                slab, at = layer // WIDTH, layer % WIDTH
                for f in range(FIELDS):
                    if slab == 1:
                        before_q = qs[f, at] if with_z else zero
                        change = z[2][3 + f, at] if with_z else zero
                        c0 = q[f] + (z7[3 + f, at] - before_q)
                        c1 = x1[f, at] + 0.5 * ((q[f] - before_q) + change)
                        odd_pair[0, f, at] = c0
                        odd_pair[1, f, at] = c1
                        if masses[f]:
                            middle[f, layer] = c0 - 0.25 * c1
                    elif masses[f]:
                        y = z[slab + 1][3 + f, at] if with_z else zero
                        middle[f, layer] = 0.875 * q[f] + y + zo[slab][f, at]

            def emit_even(layer, q):
                for f in range(FIELDS):
                    c0 = q[f] + o[0, f, layer]
                    c1 = 0.5 * (q[f] + odd_pair[0, f, layer]) + o[1, f, layer]
                    change = c0 - even[0, f, layer]
                    even_pair[0, f, layer] = c0
                    even_pair[1, f, layer] = c1
                    if final:
                        continue
                    z7_out[3 + f, layer] = change
                    if masses[f]:
                        carried = c0 - 0.25 * c1
                        z3[f, layer] = carried
                        z6[f, layer] = carried
                        z7_out[f, layer] = carried
                        z6[3 + f, layer] = -0.875 * qa[f, layer] - 0.125 * change

            if with_z:
                right = masses_only(z)
            else:
                right = lambda f, layer: zero if masses[f] else None
            middle_at = lambda f, layer: middle[f, layer] if masses[f] else None
            inv_at = lambda f, layer: even[2 + layer // WIDTH, f, layer % WIDTH]
            solve(stencil, right, layers_of(iv), 5 * WIDTH, scratch, emit_odd)
            solve(stencil, middle_at, inv_at, 3 * WIDTH, scratch, emit_even)

    spec = pl.BlockSpec(memory_space=pltpu.VMEM)
    operands = [place] + (list(arrived) if with_z else []) + list(inv_five) + [pack]
    operands += list(own_three) + list(pair) + [offset, ahead]
    operands += [solved] if with_z else []
    operands += list(done) if with_done else []
    operands += list(grad) if with_grad else []
    operands += [mark] if mark is not None else []
    outs = [(2,) + SLAB, (2,) + SLAB] + ([SLAB] if with_grad else [])
    outs += [] if final else [carry(3), carry(6), carry(7)]
    return pl.pallas_call(
        body,
        in_specs=[pl.BlockSpec(memory_space=pltpu.SMEM)] + [spec] * (len(operands) - 1),
        out_specs=[spec] * len(outs),
        out_shape=[jax.ShapeDtypeStruct(shape, jnp.float32) for shape in outs],
        scratch_shapes=[vmem((3, 3 * WIDTH, 8, 128))] + [vmem((FIELDS, 5 * WIDTH, 8, 128))] * 3,
        compiler_params=pltpu.CompilerParams(vmem_limit_bytes=24 * 1024 * 1024),
        cost_estimate=pl.CostEstimate(flops=88 * 4 * 1024 * 20, bytes_accessed=1 << 20, transcendentals=0),
    )(*operands)


def routes(times, slabs, moved, chosen=None):
    pairs = []
    for k in range(times):
        for s in range(slabs):
            target = moved(k, s)
            if target is None or (chosen is not None and not chosen(k)):
                continue
            k2, s2 = target
            if 0 <= k2 < times and 0 <= s2 < slabs:
                pairs.append((k * slabs + s, k2 * slabs + s2))
    return pairs


def send(value, pairs):
    return lax.ppermute(value, AXES, pairs)


def program(times, slabs):
    chips = times // 2

    def shift(count):
        return routes(times, slabs, lambda k, s: (k, s + count))

    right_one, left_one = shift(1), shift(-1)
    earlier = routes(times, slabs, lambda k, s: (k - 1, s))
    even_to_odd = routes(times, slabs, lambda k, s: (k + 1, s), lambda k: k % 2 == 0)
    swap = routes(times, slabs, lambda k, s: (k ^ 1, s))
    odd_to_even = routes(times, slabs, lambda k, s: (k - 1, s), lambda k: k % 2 == 1)
    reach = (2, 1, 0, -1, -2)
    odd, even = (lambda k: k % 2 == 1), (lambda k: k % 2 == 0)
    odd_right, odd_left = (routes(times, slabs, lambda k, s, d=d: (k, s + d), odd) for d in (1, -1))
    later = routes(times, slabs, lambda k, s: (k + 2, s), odd)
    sooner = routes(times, slabs, lambda k, s: (k - 2, s), odd)

    def hop_routes(hop):
        group = [h for h in range(1, chips) if (h - hop) % 4 == 0]
        senders = [2 * (chips - h) + 1 for h in group]
        return [
            routes(times, slabs, lambda k, s, d=d: (k - 2, s + d), lambda k: k in senders)
            for d in reach
        ]

    def on_device(forward_states, adjoint_source, source_gain, guess_pairs):
        states = forward_states.astype(jnp.float32)
        ahead = send(guess_pairs[0], earlier)
        inverses = [1.0 / make_diagonal(states[n], source_gain, fine_rate) for n in range(4)]
        coarse = 1.0 / make_diagonal(states[0], source_gain, coarse_rate)
        right = adjoint_source[3] + column(masses) * (4.0 * ahead[0] - ahead[1])
        up = down = jnp.concatenate([right, inverses[3], coarse])
        previous, total = ahead[0], None
        exchanged = []
        for n in (3, 2, 1, 0):
            low, high = send(up, right_one), send(down, left_one)
            exchanged.append((low, up, high))
            if n:
                rest = dict(source=adjoint_source[n - 1], factor=inverses[n - 1])
            else:
                rest = dict(coarse=exchanged[0])
            step = fine_step(n, up, low, high, states[n], previous, total, **rest)
            if n:
                previous, total, up, *more = step
                down = more[0] if more else up
        (low, own, high), (low_two, _, high_two) = exchanged[:2]
        inv_five = [part[2 * FIELDS :] for part in (low_two, low, own, high, high_two)]
        total, z7, pack = step

        prior = send(jnp.stack([part[2 * FIELDS :] for part in (low, own, high)]), later)
        pack = send(pack, swap)
        grad = total + pack[5]
        both = jnp.concatenate([z7[:3], pack[0, :3] - 0.25 * pack[1, :3]])
        own_three = (send(both, odd_right), both, send(both, odd_left))
        offset, before = offsets_step(pack, *own_three, z7, prior)
        solved = send(before, sooner)

        place = (lax.axis_index("tm").astype(jnp.int32)).reshape(1)
        is_even = lax.axis_index("tm") % 2 == 0
        stages = []
        far = 1
        while far < chips:
            stages.append(routes(times, slabs, lambda k, s, d=far: (2 * ((k // 2) ^ d), s), even))
            far *= 2
        stages.append(even_to_odd)
        arrived, done = None, None
        for hop in range(max(chips, len(stages) + 1)):
            added, mark = None, None
            if hop and hop < chips:
                arrived = [send(part, path) for part, path in zip(payload, hop_routes(hop))]
                mark = sum(part[:1] if part.shape[0] < 4 else part[:4] for part in arrived)
            if hop and stages:
                received = send(jnp.where(place[0] < 0, mark, grad), stages.pop(0))
                mark = None
                added = (grad if stages else jnp.where(is_even, grad, 0.0), received)
            if hop < chips:
                odd_pair, even_pair, *more = chip_step(
                    times - 1 - 2 * hop, place, arrived, inv_five, pack, own_three, (z7, previous),
                    offset, before, solved if hop else None, done, added, mark,
                )
                if added:
                    grad = more.pop(0)
                if hop < chips - 1:
                    z3, z6, z7_out = more
                    if not hop:
                        z3, z6, z7_out = (jnp.where(place[0] < 0, solved[:1], p) for p in more)
                    payload = (z3, z6, z7_out, z6, z3)
                done = (odd_pair, even_pair)
            elif added:
                grad = added[0] + added[1]

        corrected = jnp.where(is_even, send(done[1], odd_to_even), done[0])
        return corrected[None], grad

    return on_device


def solution(mesh):
    placed = (
        P("tm", None, "space", None, None),
        P("tm", None, "space", None, None),
        P(None, "space", None, None),
        P("tm", None, None, "space", None, None),
    )
    return jax.shard_map(
        program(mesh.shape["tm"], mesh.shape["space"]),
        mesh=mesh,
        in_specs=placed,
        out_specs=(P("tm", None, None, "space", None, None), P(None, "space", None, None)),
        check_vma=False,
    )
```
